256 devices in a mesh: ctx: 16 (over z_lo, y), fsdp: 16 (over z_hi, x, core).
Axes of the slice: x: 4, y: 4, z: 8 (z_hi: 2, z_lo: 4; z = z_hi * 4 + z_lo), core: 2. Of those that a mesh axis runs over, the one named last changes fastest.
Arguments:
- hidden_in: bfloat16 [16, 1024, 7168], P('fsdp', 'ctx'), may hold values from -4 to 4
- queries: bfloat16 [16, 1024, 18432], P('fsdp', 'ctx'), may hold values from -18 to 18
- span_latent: bfloat16 [16, 1024, 576], P('fsdp', 'ctx'), may hold values from -7 to 7
- cache_latent: bfloat16 [16, 1024, 576], P('fsdp', 'ctx'), may hold values from -4 to 4
- cache_len: int32 [16, 16], P('fsdp'), may hold values from 1 to 64, 512 in all within a row
- value_up: bfloat16 [32, 512, 128], P('ctx'), may hold values from -1 to 1
- out_proj: bfloat16 [7168, 4096], P('fsdp', 'ctx'), may hold values from -0.09375 to 0.09375
- norm_gain: float32 [7168], replicated, may hold values from 0.5 to 2
- expert_gate: bfloat16 [7168, 4096], P('fsdp', 'ctx'), may hold values from -0.0625 to 0.0625
- expert_up: bfloat16 [7168, 4096], P('fsdp', 'ctx'), may hold values from -0.0625 to 0.0625
- expert_down: bfloat16 [7168, 4096], P('fsdp', 'ctx'), may hold values from -0.125 to 0.125
- routes: int32 [16, 1024, 8], P('fsdp'), may hold values from 0 to 383, as said below
- route_weights: float32 [16, 1024, 8], P('fsdp'), may hold values from 0.2 to 1
Outputs:
- layer_out: bfloat16 [16, 1024, 7168], P('fsdp', 'ctx')
The draws below stay inside these ranges and needn't reach their ends.
Inputs may be any that keep to these rules, and one draw needn't show every extreme that they name: `routes`: each token names 8 different experts. Each expert below 2 is named by at most 4 of the 64 tokens of one span slice, and by exactly 4 in some slice of every sequence.
All inputs are finite; a program needn't handle non-finite values.
Results may differ from the reference program's by a relative error of at most 0.023.
Values may be sent and summed in bfloat16 or wider, within the bound.
A program may use at most 128 MiB of HBM per device.

```python
import math
import jax
import jax.numpy as jnp
import numpy as np
from jax import lax

D = 7168
HEADS = 32
LATENT = 512
ROPE = 64
VHEAD = 128
FF_EXP = 2048
EXPERTS = 384
TOPK = 8
HID_DEV = 256
CAP = 4
Q_DEV = 64
CACHE_DEV = 64
EXP_FLIGHT = 2
SEQS = 16
SPAN = 1024
CACHE_ALL = 1024
N_CTX = 16


def draw_queries(key, part):
    key = jax.random.fold_in(key, 11)
    array_shape = (SEQS, SPAN, HEADS, LATENT + ROPE)
    values = jnp.clip(jax.random.normal(key, array_shape, jnp.float32), -4.0, 4.0)
    return values.reshape(SEQS, SPAN, HEADS * (LATENT + ROPE)).astype(jnp.bfloat16)


def draw_span_latent(key, part):
    key = jax.random.fold_in(key, 23)
    array_shape = (SEQS, SPAN, LATENT + ROPE)
    values = jnp.clip(jax.random.normal(key, array_shape, jnp.float32), -4.0, 4.0)
    return values.astype(jnp.bfloat16)


def draw_routes(key, part):
    key = jax.random.fold_in(key, 37)
    subkeys = jax.random.split(key, 5)
    blocks = SEQS * N_CTX
    row_total = blocks * Q_DEV
    others = EXPERTS - EXP_FLIGHT
    ranking = jax.random.randint(subkeys[0], (row_total, others), 0, 1 << 20) * 1024 + jnp.arange(others, dtype=jnp.int32)
    chosen = lax.top_k(ranking, TOPK)[1].astype(jnp.int32) + EXP_FLIGHT
    loads = jax.random.randint(subkeys[1], (SEQS, N_CTX, EXP_FLIGHT), 1, CAP + 1)
    forced = jax.random.randint(subkeys[2], (SEQS, 1, EXP_FLIGHT), 0, N_CTX)
    loads = jnp.where(jnp.arange(N_CTX)[None, :, None] == forced, CAP, loads).reshape(blocks, EXP_FLIGHT)
    shuffle = jax.random.randint(subkeys[3], (blocks, Q_DEV), 0, 1 << 20) * 1024 + jnp.arange(Q_DEV, dtype=jnp.int32)
    placing = jnp.argsort(jnp.argsort(shuffle, axis=1), axis=1).astype(jnp.int32)
    expert_of = placing // CAP
    in_window = expert_of < EXP_FLIGHT
    load_of = jnp.take_along_axis(loads, jnp.minimum(expert_of, EXP_FLIGHT - 1), axis=1)
    assigned = (in_window & (placing % CAP < load_of)).reshape(row_total)
    column = jax.random.randint(subkeys[4], (row_total, 1), 0, TOPK)
    routed = jnp.where(assigned[:, None] & (jnp.arange(TOPK)[None, :] == column), expert_of.reshape(row_total)[:, None], chosen)
    return routed.reshape(SEQS, SPAN, TOPK).astype(jnp.int32)


def levels(key, dims, shards, smallest, high):
    gain = 1.0
    for dim, blocks in shards:
        steps = jax.random.uniform(jax.random.fold_in(jax.random.fold_in(key, 6), dim), (blocks,), jnp.float32, smallest / len(shards), high / len(shards))
        gain = gain * jnp.repeat(jnp.exp(steps), dims[dim] // blocks).reshape((-1,) + (1,) * (len(dims) - 1 - dim))
    return gain


def split_up(number_of, total, most, slope):
    weights = [(1 << 20) // math.isqrt(standing ** slope) + 1 for standing in range(2, number_of + 1)]
    surplus, counts = total - most - (number_of - 1), [1] * (number_of - 1)
    while surplus > 0:
        movable = [i for i in range(number_of - 1) if counts[i] < most]
        mass, budget = sum([weights[i] for i in movable]), surplus
        for i in movable:
            more = min(most - counts[i], max(1, budget * weights[i] // mass), surplus)
            counts[i] = counts[i] + more
            surplus = surplus - more
    return np.array([most] + counts)


def uneven(key, number_of, total, most, slope):
    if number_of == 2:
        one = jax.random.randint(key, (), max(1, total - most), min(most, total - 1) + 1)
        return jnp.stack([one, total - one])
    tallies = jnp.asarray(split_up(number_of, total, most, slope), jnp.int32)
    twos = (number_of - 1) // 2
    source_of, sink = tallies[1:1 + 2 * twos:2], tallies[2:2 + 2 * twos:2]
    margin = jnp.minimum(source_of - 1, most - sink)
    shifted = jax.random.randint(jax.random.fold_in(key, 1), (twos,), 0, 1 << 20) % (margin + 1)
    tallies = tallies.at[1:1 + 2 * twos:2].set(source_of - shifted).at[2:2 + 2 * twos:2].set(sink + shifted)
    return tallies[jax.random.permutation(jax.random.fold_in(key, 2), number_of)]


def normal_values(stream_key, shape, spread, most, shards=(), kind=jnp.bfloat16):
    factor_of = levels(stream_key, shape, shards, -0.22, 0.18) if shards else 1.0
    drawn = jax.random.normal(stream_key, shape, jnp.float32) * spread * factor_of
    return jnp.minimum(jnp.maximum(drawn, -most), most).astype(kind)


def setup_inputs(seed: int = 0) -> dict:
    streams_of = jax.random.split(jax.random.key(seed), 14)
    hidden_in = normal_values(streams_of[0], (SEQS, SPAN, D), 0.5, 4.0, ((0, 16), (1, 16)))
    queries = draw_queries(jax.random.fold_in(streams_of[13], 71), 0)
    span_latent = draw_span_latent(jax.random.fold_in(streams_of[13], 71), 0)
    cache_latent = normal_values(streams_of[3], (SEQS, CACHE_ALL, LATENT + ROPE), 1.0, 4.0, ((0, 16), (1, 16)))
    cache_len = jax.vmap(lambda own: uneven(own, N_CTX, N_CTX * CACHE_DEV // 2, CACHE_DEV, 2))(jax.random.split(streams_of[4], SEQS)).reshape((SEQS, N_CTX)).astype(jnp.int32)
    value_up = normal_values(streams_of[5], (HEADS, LATENT, VHEAD), 32 ** -0.5, 1.0, ((0, 16),))
    out_proj = normal_values(streams_of[6], (D, HEADS * VHEAD), (HEADS * VHEAD) ** -0.5, 0.09375, ((0, 16), (1, 16)))
    norm_gain = jnp.clip(jax.random.uniform(streams_of[7], (D,), jnp.float32, 0.5, 2.0), 0.5, 2.0)
    expert_gate = normal_values(streams_of[8], (D, EXP_FLIGHT * FF_EXP), D ** -0.5, 0.0625, ((0, 16), (1, 16)))
    expert_up = normal_values(streams_of[9], (D, EXP_FLIGHT * FF_EXP), D ** -0.5, 0.0625, ((0, 16), (1, 16)))
    expert_down = normal_values(streams_of[10], (D, EXP_FLIGHT * FF_EXP), FF_EXP ** -0.5, 0.125, ((0, 16), (1, 16)))
    routes = draw_routes(jax.random.fold_in(streams_of[13], 71), 0)
    route_weights = jnp.clip(0.2 + 0.8 * jax.random.uniform(streams_of[12], (SEQS, SPAN, TOPK), jnp.float32) ** levels(streams_of[12], (SEQS, SPAN, TOPK), ((0, 16),), -0.2, 0.2), 0.2, 1.0)
    return {"hidden_in": hidden_in, "queries": queries, "span_latent": span_latent, "cache_latent": cache_latent, "cache_len": cache_len, "value_up": value_up, "out_proj": out_proj, "norm_gain": norm_gain, "expert_gate": expert_gate, "expert_up": expert_up, "expert_down": expert_down, "routes": routes, "route_weights": route_weights}


SOFTMAX_SCALE = 192.0 ** (-0.5)
EPSILON = 1e-06
NEGATIVE = -1e+30
FAR_RANK = 1 << 30

def window_slots(routed, weighted):
    expert_ids = jnp.arange(EXP_FLIGHT, dtype=jnp.int32)
    matched = routed[:, :, None] == expert_ids[None, None, :]
    hitting = jnp.any(matched, axis=1).astype(jnp.int32)
    gate_token = lax.optimization_barrier(jnp.sum(jnp.where(matched, weighted[:, :, None], 0.0), axis=1))
    blocked = hitting.reshape(N_CTX, Q_DEV, EXP_FLIGHT)
    within = (jnp.cumsum(blocked, axis=1) - blocked).astype(jnp.int32)
    slot_row = (jnp.arange(N_CTX, dtype=jnp.int32)[:, None, None] * CAP + within).reshape(SPAN, EXP_FLIGHT)
    slot_ids = jnp.arange(N_CTX * CAP, dtype=jnp.int32)
    selector = (slot_row.T[:, None, :] == slot_ids[None, :, None]) & (hitting.T[:, None, :] == 1)
    gate_slot = lax.optimization_barrier(jnp.sum(jnp.where(selector, gate_token.T[:, None, :], 0.0), axis=2))
    return (selector, gate_slot)

def reference(hidden_in, queries, span_latent, cache_latent, cache_len, value_up, out_proj, norm_gain, expert_gate, expert_up, expert_down, routes, route_weights):
    group = HEADS // N_CTX
    span_pos = jnp.arange(SPAN, dtype=jnp.int32)
    cache_slots = jnp.arange(CACHE_ALL, dtype=jnp.int32)
    block_ids = jnp.arange(N_CTX, dtype=jnp.int32)

    def one_sequence(seq_index):
        residual = hidden_in[seq_index]
        query_all = queries[seq_index].reshape(SPAN, HEADS, LATENT + ROPE)
        lengths = cache_len[seq_index]
        owner_block = cache_slots // CACHE_DEV
        length_at = lax.optimization_barrier(jnp.sum(jnp.where(owner_block[:, None] == block_ids[None, :], lengths[None, :], 0), axis=1))
        live = cache_slots % CACHE_DEV < length_at
        key_rank = jnp.concatenate([jnp.where(live, -1, FAR_RANK).astype(jnp.int32), span_pos])
        key_rows = jnp.concatenate([cache_latent[seq_index], span_latent[seq_index]], axis=0)
        visible = key_rank[None, :] <= span_pos[:, None]

        def one_head(head):
            query_head = lax.dynamic_index_in_dim(query_all, head, 1, keepdims=False)
            scores = jnp.dot(query_head, key_rows.T, preferred_element_type=jnp.float32) * SOFTMAX_SCALE
            scores = jnp.where(visible, scores, NEGATIVE)
            highest = lax.optimization_barrier(jnp.max(scores, axis=1, keepdims=True))
            exp_terms = jnp.where(visible, jnp.exp(scores - highest), 0.0)
            denominator = lax.optimization_barrier(jnp.sum(exp_terms, axis=1, keepdims=True))
            attended = (jnp.dot(exp_terms.astype(jnp.bfloat16), key_rows[:, :LATENT], preferred_element_type=jnp.float32) / denominator).astype(jnp.bfloat16)
            value_map = lax.dynamic_index_in_dim(value_up, head, 0, keepdims=False)
            return jnp.dot(attended, value_map, preferred_element_type=jnp.float32).astype(jnp.bfloat16)
        head_out = lax.map(one_head, jnp.arange(HEADS, dtype=jnp.int32))
        flat_out = jnp.transpose(head_out, (1, 0, 2)).reshape(SPAN, HEADS * VHEAD)
        mixed = residual.astype(jnp.float32) + jnp.dot(flat_out, out_proj.T, preferred_element_type=jnp.float32)
        selector, gate_slot = window_slots(routes[seq_index], route_weights[seq_index])
        row_index = lax.optimization_barrier(jnp.sum(jnp.where(selector, span_pos[None, None, :], 0), axis=2)).astype(jnp.int32)
        occupied = jnp.any(selector, axis=2)
        slot_rows = mixed[row_index] * occupied[:, :, None]
        mean_square = lax.optimization_barrier(jnp.mean(slot_rows * slot_rows, axis=2, keepdims=True))
        normed = (slot_rows * lax.rsqrt(mean_square + EPSILON) * norm_gain).astype(jnp.bfloat16)
        activated = []
        for expert in range(EXP_FLIGHT):
            gate_cols = expert_gate[:, expert * FF_EXP:(expert + 1) * FF_EXP]
            up_cols = expert_up[:, expert * FF_EXP:(expert + 1) * FF_EXP]
            gate_proj = jnp.dot(normed[expert], gate_cols, preferred_element_type=jnp.float32)
            up_proj = jnp.dot(normed[expert], up_cols, preferred_element_type=jnp.float32)
            activated.append((jax.nn.silu(gate_proj) * up_proj).astype(jnp.bfloat16))
        act_all = jnp.concatenate(activated, axis=1)

        def add_group(running, group_index):
            head_cols = lax.dynamic_slice_in_dim(flat_out, group_index * group * VHEAD, group * VHEAD, 1)
            proj_cols = lax.dynamic_slice_in_dim(out_proj, group_index * group * VHEAD, group * VHEAD, 1)
            group_term = jnp.dot(head_cols, proj_cols.T, preferred_element_type=jnp.float32)
            expert = group_index * HID_DEV // FF_EXP
            act_rows = lax.dynamic_slice_in_dim(act_all, group_index * HID_DEV, HID_DEV, 1)
            down_slice = lax.dynamic_slice_in_dim(expert_down, group_index * HID_DEV, HID_DEV, 1)
            gate_here = lax.dynamic_index_in_dim(gate_slot, expert, 0, keepdims=False)
            occupied_here = lax.dynamic_index_in_dim(occupied, expert, 0, keepdims=False)
            rows_here = lax.dynamic_index_in_dim(row_index, expert, 0, keepdims=False)
            slot_values = jnp.dot(act_rows, down_slice.T, preferred_element_type=jnp.float32) * gate_here[:, None]
            slot_values = slot_values * occupied_here[:, None]
            group_term = group_term + jnp.zeros((SPAN, D), jnp.float32).at[rows_here].add(slot_values)
            rounded = lax.optimization_barrier(group_term.astype(jnp.bfloat16))
            return (running + rounded.astype(jnp.float32), None)
        summed, unused = lax.scan(add_group, residual.astype(jnp.float32), jnp.arange(N_CTX, dtype=jnp.int32))
        return summed.astype(jnp.bfloat16)
    return lax.map(one_sequence, jnp.arange(SEQS, dtype=jnp.int32))
```

```python
import functools

import jax
import jax.numpy as jnp
from jax import lax
from jax.experimental import pallas as pl
from jax.experimental.pallas import tpu as pltpu
from jax.sharding import PartitionSpec as P

MESH = pl.DeviceIdType.MESH
F32 = jnp.float32
BF16 = jnp.bfloat16

CAP = 4
SCALE_LOG2 = 192.0 ** (-0.5) * 1.4426950408889634
EPSILON = 1e-06
NEGATIVE = -1e30
N_SEND = 128
N_RECV = 128


def dot_nt(a, b):
    return lax.dot_general(a, b, (((1,), (1,)), ((), ())), preferred_element_type=F32)


def dot_nn(a, b):
    return jnp.dot(a, b, preferred_element_type=F32)


class Links:
    def __init__(self, send, recv):
        self.send, self.recv = send, recv
        self.n_send = self.n_recv = 0
        self.open = []

    def new_recv(self, count=1):
        base = self.n_recv
        self.n_recv += count
        assert self.n_recv <= N_RECV
        return base

    def start(self, src, dst, recv_index, device):
        copy = pltpu.make_async_remote_copy(
            src_ref=src,
            dst_ref=dst,
            send_sem=self.send.at[self.n_send],
            recv_sem=self.recv.at[recv_index],
            device_id=device,
            device_id_type=MESH,
        )
        self.n_send += 1
        assert self.n_send <= N_SEND
        copy.start()
        self.open.append(copy)

    def arrived(self, dst, recv_index, device):
        pltpu.make_async_remote_copy(
            src_ref=dst,
            dst_ref=dst,
            send_sem=self.send.at[0],
            recv_sem=self.recv.at[recv_index],
            device_id=device,
            device_id_type=MESH,
        ).wait_recv()

    def finish(self):
        for copy in self.open:
            copy.wait_send()


class Ring:
    def __init__(self, links, at, device, chunk, half):
        self.links, self.at, self.device = links, at, device
        self.chunk, self.half = chunk, half
        self.base = links.new_recv(4)
        self.up, self.down, self.far = (lax.rem(at + i, 4) for i in (1, 3, 2))

    def start(self):
        own = self.chunk(self.at)
        self.links.start(own, own, self.base, self.device(self.up))
        self.links.start(own, own, self.base + 1, self.device(self.down))

    def forward(self):
        self.links.arrived(self.chunk(self.down), self.base, self.device(self.down))
        part = self.half(self.down, 0)
        self.links.start(part, part, self.base + 2, self.device(self.up))
        self.links.arrived(self.chunk(self.up), self.base + 1, self.device(self.up))
        part = self.half(self.up, 1)
        self.links.start(part, part, self.base + 3, self.device(self.down))

    def finish(self):
        self.links.arrived(self.half(self.far, 0), self.base + 2, self.device(self.down))
        self.links.arrived(self.half(self.far, 1), self.base + 3, self.device(self.up))


def kernel(
    lens, hid, q, span, cache, gain, route_row, weight_row,
    vu_in, wo_in, wg_in, wu_in, wd_in,
    out,
    kb, kc, qs, vbuf, wbuf, wo, att, ho, hb,
    part, rsa, rsb, zsend, zrecv, mixed, normed,
    sb, sblk, yb, dp, dpa, dpb, zb, zr,
    send_sems, recv_sems, local_sems,
):
    c, f = lax.axis_index("ctx"), lax.axis_index("fsdp")
    z, y = c // 4, lax.rem(c, 4)
    zh, x, k = f // 8, lax.rem(f // 2, 4), lax.rem(f, 2)
    zm = lax.rem(z, 2)
    expert = z // 2
    links = Links(send_sems, recv_sems)

    def at_z(z2):
        return {"ctx": z2 * 4 + y, "fsdp": f}

    def at_y(y2):
        return {"ctx": z * 4 + y2, "fsdp": f}

    def at_x(x2):
        return {"ctx": c, "fsdp": zh * 8 + x2 * 2 + k}

    def at_zh(z2, zh2):
        return {"ctx": z2 * 4 + y, "fsdp": zh2 * 8 + x * 2 + k}

    other_core = {"ctx": c, "fsdp": zh * 8 + x * 2 + (1 - k)}
    far_half = at_zh(z, 1 - zh)
    pair = at_z(z + 1 - 2 * zm)
    zs = [lax.rem(z + i, 4) for i in range(4)]
    ys = [lax.rem(y + i, 4) for i in range(4)]
    xs = [lax.rem(x + i, 4) for i in range(4)]

    local = []

    def place(src, dst):
        copy = pltpu.make_async_copy(src, dst, local_sems.at[len(local)])
        copy.start()
        local.append(copy)

    place(cache, kb.at[0, c])
    place(span, kb.at[1, c])
    place(vu_in.at[k, pl.ds(pl.multiple_of(x * 128, 128), 128)], vbuf.at[k, x, z, y])
    for i, ref in enumerate((wg_in, wu_in, wd_in)):
        place(ref, wbuf.at[i, zh, x, k])

    barrier = pltpu.get_barrier_semaphore()
    peers = [at_y(ys[i]) for i in (1, 2, 3)] + [at_x(xs[i]) for i in (1, 2, 3)] + [other_core]
    peers += [at_zh(zs[i], zh) for i in (1, 2, 3)] + [at_zh(zs[i], 1 - zh) for i in range(4)]
    for peer in peers:
        pl.semaphore_signal(barrier, inc=1, device_id=peer, device_id_type=MESH)
    pl.semaphore_wait(barrier, len(peers))
    for copy in local:
        copy.wait()

    keys_z = links.new_recv(3)
    for i in (1, 2, 3):
        links.start(kb.at[:, c], kb.at[:, c], keys_z + i - 1, at_z(zs[i]))
    keys_y = []
    for i in range(4):
        zi = zs[i]
        keys_y.append(
            Ring(
                links, y, at_y,
                lambda o, zi=zi: kb.at[:, zi * 4 + o],
                lambda o, j, zi=zi: kb.at[j, zi * 4 + o],
            )
        )
    keys_y[0].start()
    vu_z = links.new_recv(3)
    for i in (1, 2, 3):
        own = vbuf.at[k, x, z, y]
        links.start(own, own, vu_z + i - 1, at_z(zs[i]))
    vu_y = Ring(
        links, y, at_y,
        lambda o: vbuf.at[k, x, :, o],
        lambda o, j: vbuf.at[k, x, pl.ds(2 * j, 2), o],
    )
    vu_x = Ring(
        links, x, at_x,
        lambda o: vbuf.at[k, o],
        lambda o, j: vbuf.at[k, o, pl.ds(2 * j, 2)],
    )
    gud_x = [
        Ring(
            links, x, at_x,
            lambda o, h=h: wbuf.at[:, h, o, k],
            lambda o, j, h=h: wbuf.at[:, h, o, k, pl.ds(224 * j, 224)],
        )
        for h in (zh, 1 - zh)
    ]
    gud_x[0].start()
    out_x = Ring(
        links, x, at_x,
        lambda o: wo.at[:, o, k],
        lambda o, j: wo.at[pl.ds(2 * j, 2), o, k],
    )

    def relayout(index, carry):
        zq, yq = index // 4, lax.rem(index, 4)
        cols = q[:, pl.ds(pl.multiple_of(index * 1152, 128), 1152)]
        qs[yq, zq, 0] = cols[:, :576]
        qs[yq, zq, 1] = cols[:, 576:]
        return carry

    lax.fori_loop(0, 8, relayout, 0)

    for i in (1, 2, 3):
        links.arrived(kb.at[:, zs[4 - i] * 4 + y], keys_z + i - 1, at_z(zs[4 - i]))
        keys_y[4 - i].start()

    out_z = links.new_recv(4)
    out_sends = []
    for a in range(2):
        for b in range(2):
            z2 = zh + 2 * a
            own = (z2 == z) & (zh == b)
            sem = links.n_send
            links.n_send += 1

            def remote(sem=sem, z2=z2, b=b):
                return pltpu.make_async_remote_copy(
                    src_ref=wo_in,
                    dst_ref=wo.at[z, x, k],
                    send_sem=send_sems.at[sem],
                    recv_sem=recv_sems.at[out_z + z],
                    device_id=at_zh(z2, b),
                    device_id_type=MESH,
                )

            @pl.when(own)
            def _():
                pltpu.make_async_copy(wo_in, wo.at[z, x, k], recv_sems.at[out_z + z]).start()

            @pl.when(jnp.logical_not(own))
            def _():
                remote().start()

            out_sends.append((own, remote))

    for i in (1, 2, 3):
        links.arrived(vbuf.at[k, x, zs[4 - i], y], vu_z + i - 1, at_z(zs[4 - i]))
    vu_y.start()

    lax.fori_loop(8, 16, relayout, 0)

    order = (0, 3, 2, 1)
    for i in order:
        keys_y[i].forward()
    vu_y.forward()
    for i in order:
        keys_y[i].finish()
    vu_y.finish()
    vu_x.start()
    gud_x[0].forward()

    slot = lax.broadcasted_iota(jnp.int32, (512, 128), 0)
    lane = lax.broadcasted_iota(jnp.int32, (512, 128), 1)
    packed = None
    first = 0
    for b in range(0, 16, 2):
        len0, len1 = lens[0, b], lens[0, b + 1]
        left = (lane < len0) & (slot == lane + first)
        right = (lane >= 64) & (lane < 64 + len1) & (slot == lane - 64 + (first + len0))
        pick = jnp.where(left & (lane < 64) | right, 1.0, 0.0).astype(BF16)
        term = dot_nn(pick, kb[0, pl.ds(b, 2)].reshape(128, 576))
        packed = term if packed is None else packed + term
        first = first + len0 + len1
    kc[...] = packed.astype(BF16)

    def attend(group):
        def step(half, carry):
            rows = qs[group, pl.ds(2 * half, 2)].reshape(256, 576)
            s1 = dot_nt(rows, kc[...])
            s2 = dot_nt(rows, kb[1].reshape(1024, 576))
            token = lax.rem(lax.broadcasted_iota(jnp.int32, (256, 1024), 0), 64)
            key = lax.broadcasted_iota(jnp.int32, (256, 1024), 1)
            s2 = jnp.where(key <= token + c * 64, s2, NEGATIVE)
            top = jnp.maximum(
                jnp.max(s1, axis=1, keepdims=True), jnp.max(s2, axis=1, keepdims=True)
            )
            p1 = jnp.exp2((s1 - top) * SCALE_LOG2)
            p2 = jnp.exp2((s2 - top) * SCALE_LOG2)
            total = jnp.sum(p1, axis=1, keepdims=True) + jnp.sum(p2, axis=1, keepdims=True)
            acc = dot_nn(p1.astype(BF16), kc[:, :512])
            acc = acc + dot_nn(p2.astype(BF16), kb[1, :, :, :512].reshape(1024, 512))
            att[group, pl.ds(2 * half, 2)] = (acc / total).astype(BF16).reshape(2, 2, 64, 512)
            return carry

        lax.fori_loop(0, 2, step, 0)

    attend(ys[1])
    for i in range(4):
        links.arrived(wo.at[i, x, k], out_z + i, at_z(zs[1]))
    out_x.start()
    out_core = links.new_recv(4)
    links.start(wo.at[:, x, k], wo.at[:, x, k], out_core, other_core)
    gud_z = links.new_recv(1)
    mine = wbuf.at[:, zh, x, k]
    links.start(mine, mine, gud_z, far_half)

    attend(ys[2])
    vu_x.forward()
    attend(ys[3])
    vu_x.finish()
    vu_core = links.new_recv(1)
    links.start(vbuf.at[k], vbuf.at[k], vu_core, other_core)
    attend(ys[0])
    out_x.forward()
    for i in (1, 3):
        links.start(wo.at[:, xs[i], k], wo.at[:, xs[i], k], out_core + i, other_core)
    gud_x[0].finish()
    gud_core = links.new_recv(2)
    ready = wbuf.at[:, zh, :, k]
    links.start(ready, ready, gud_core, other_core)
    links.arrived(vbuf.at[1 - k], vu_core, other_core)

    ho_y = links.new_recv(4)
    for i in (1, 2, 3, 0):
        group = ys[i]
        for zq in range(4):
            pieces = []
            for j in range(2):
                value = jnp.concatenate([vbuf[j, r, zq, group] for r in range(4)], axis=0)
                pieces.append(dot_nn(att[group, zq, j], value).astype(BF16))
            ho[i, :, zq * 256 : (zq + 1) * 256] = jnp.concatenate(pieces, axis=1)
        if i:
            links.start(ho.at[i], hb.at[y, zm], ho_y + i, at_y(group))
        else:
            hb[y, zm] = ho[0]
    ho_z = links.new_recv(4)
    links.start(ho.at[0], hb.at[y, zm], ho_z, pair)
    for i in (1, 2, 3):
        source = ys[4 - i]
        links.arrived(hb.at[source, zm], ho_y + i, at_y(source))
        links.start(hb.at[source, zm], hb.at[source, zm], ho_z + i, pair)
    out_x.finish()
    links.start(wo.at[:, xs[2], k], wo.at[:, xs[2], k], out_core + 2, other_core)
    for i in range(4):
        source = ys[(4 - i) % 4]
        links.arrived(hb.at[source, 1 - zm], ho_z + i, pair)

    rs_a, rs_b, rs_z = links.new_recv(8), links.new_recv(8), links.new_recv(4)
    tiles = (0, 1, 3, 2)

    def project(n):
        i = tiles[n]
        links.arrived(wo.at[:, xs[i], 1 - k], out_core + i, other_core)
        acc = None
        for zq in range(4):
            term = dot_nt(
                hb[:, :, :, zq * 256 : (zq + 1) * 256].reshape(512, 256),
                wo[zq, xs[i]].reshape(896, 256),
            )
            acc = term if acc is None else acc + term
        part[n] = acc.astype(BF16).reshape(4, 2, 64, 896)
        links.start(part.at[n, ys[2], 0], rsa.at[n, 0], rs_a + 2 * n, at_y(ys[1]))
        links.start(part.at[n, ys[2], 1], rsa.at[n, 1], rs_a + 2 * n + 1, at_y(ys[3]))

    def pass_on(n):
        links.arrived(rsa.at[n, 0], rs_a + 2 * n, at_y(ys[3]))
        part[n, ys[1], 0] = (part[n, ys[1], 0].astype(F32) + rsa[n, 0].astype(F32)).astype(BF16)
        links.start(part.at[n, ys[1]], rsb.at[n, 0], rs_b + 2 * n, at_y(ys[1]))
        links.arrived(rsa.at[n, 1], rs_a + 2 * n + 1, at_y(ys[1]))
        part[n, ys[3], 1] = (part[n, ys[3], 1].astype(F32) + rsa[n, 1].astype(F32)).astype(BF16)
        links.start(part.at[n, ys[3]], rsb.at[n, 1], rs_b + 2 * n + 1, at_y(ys[3]))

    def columns(half, n):
        return pl.ds(pl.multiple_of(half * 3584 + xs[tiles[n]] * 896, 128), 896)

    def collect(n):
        links.arrived(rsb.at[n, 0], rs_b + 2 * n, at_y(ys[3]))
        links.arrived(rsb.at[n, 1], rs_b + 2 * n + 1, at_y(ys[1]))

        def total(member):
            return (
                part[n, y, member].astype(F32)
                + rsb[n, 0, member].astype(F32)
                + rsb[n, 1, member].astype(F32)
            )

        zsend[n] = total(1 - zm).astype(BF16)
        links.start(zsend.at[n], zrecv.at[n], rs_z + n, pair)
        cols = columns(zm, n)
        mixed[:, cols] = hid[:, cols].astype(F32) + total(zm)

    project(0)
    project(1)
    pass_on(0)
    links.arrived(wbuf.at[:, 1 - zh, x, k], gud_z, far_half)
    gud_x[1].start()
    project(2)
    pass_on(1)
    collect(0)
    project(3)
    pass_on(2)
    collect(1)
    pass_on(3)
    collect(2)
    collect(3)
    for n in range(4):
        links.arrived(zrecv.at[n], rs_z + n, pair)
        cols = columns(1 - zm, n)
        mixed[:, cols] = hid[:, cols].astype(F32) + zrecv[n].astype(F32)
    gud_x[1].forward()

    square = None
    for r in range(8):
        block = mixed[:, r * 896 : (r + 1) * 896]
        term = jnp.sum(block * block, axis=1, keepdims=True)
        square = term if square is None else square + term
    inverse = lax.rsqrt(square * (1.0 / 7168.0) + EPSILON)
    for r in range(8):
        cols = slice(r * 896, (r + 1) * 896)
        normed[:, cols] = (mixed[:, cols] * inverse * gain[:, cols]).astype(BF16)

    earlier = lax.broadcasted_iota(jnp.int32, (64, 64), 1) < lax.broadcasted_iota(
        jnp.int32, (64, 64), 0
    )
    earlier = jnp.where(earlier, 1.0, 0.0).astype(BF16)
    lane16 = lax.broadcasted_iota(jnp.int32, (64, 128), 1)
    chosen, gates = [], []
    for e in range(2):
        match = route_row[...] == e
        hit = jnp.sum(jnp.where(match, 1.0, 0.0), axis=1, keepdims=True)
        gates.append(jnp.sum(jnp.where(match, weight_row[...], 0.0), axis=1, keepdims=True))
        wide = jnp.broadcast_to(hit, (64, 128))
        within = dot_nn(earlier, wide.astype(BF16))
        for p in range(4):
            pick = (wide > 0.5) & (lane16 // 4 == p) & (within.astype(jnp.int32) == lax.rem(lane16, 4))
            chosen.append(jnp.where(pick, 1.0, 0.0))
    for e in range(2):
        block = None
        for p in range(4):
            pick = jnp.transpose(chosen[4 * e + p])[:16].astype(BF16)
            term = dot_nn(pick, normed[:, p * 1792 : (p + 1) * 1792])
            block = term if block is None else block + term
        sb[e] = block.astype(BF16)
    sl_z = links.new_recv(3)
    for i in (1, 2, 3):
        links.start(sb.at[zs[i] // 2], sblk.at[z], sl_z + i - 1, at_z(zs[i]))
    sblk[z] = sb[expert]
    for i in (1, 2, 3):
        links.arrived(sblk.at[zs[4 - i]], sl_z + i - 1, at_z(zs[4 - i]))
    stacked = sblk[...].reshape(64, 1792)
    row = lax.broadcasted_iota(jnp.int32, (16, 64), 0)
    col = lax.broadcasted_iota(jnp.int32, (16, 64), 1)
    same = (row // 4 == col // 16) & (lax.rem(row, 4) == lax.rem(col, 4))
    for p in range(4):
        pick = jnp.where(same & (lax.rem(col, 16) // 4 == p), 1.0, 0.0).astype(BF16)
        yb[y, p] = dot_nn(pick, stacked).astype(BF16)
    sl_y = Ring(
        links, y, at_y,
        lambda o: yb.at[o],
        lambda o, j: yb.at[o, pl.ds(2 * j, 2)],
    )
    sl_y.start()
    gud_x[1].finish()
    ready = wbuf.at[:, 1 - zh, :, k]
    links.start(ready, ready, gud_core + 1, other_core)
    sl_y.forward()
    links.arrived(wbuf.at[:, zh, :, 1 - k], gud_core, other_core)
    sl_y.finish()
    links.arrived(wbuf.at[:, 1 - zh, :, 1 - k], gud_core + 1, other_core)

    gate_acc = up_acc = None
    for p in range(4):
        rows = yb[:, p].reshape(64, 1792)
        span_x = pl.ds(2 * (p % 2), 2)
        g_term = dot_nn(rows, wbuf[0, p // 2, span_x].reshape(1792, 256))
        u_term = dot_nn(rows, wbuf[1, p // 2, span_x].reshape(1792, 256))
        gate_acc = g_term if gate_acc is None else gate_acc + g_term
        up_acc = u_term if up_acc is None else up_acc + u_term
    act = (gate_acc / (1.0 + jnp.exp(-gate_acc)) * up_acc).astype(BF16)
    for p in range(4):
        down = dot_nt(act, wbuf[2, p // 2, pl.ds(2 * (p % 2), 2)].reshape(1792, 256))
        dp[:, p] = down.astype(BF16).reshape(4, 16, 1792)

    d_a, d_b = links.new_recv(2), links.new_recv(2)
    links.start(dp.at[ys[2], pl.ds(0, 2)], dpa.at[0], d_a, at_y(ys[1]))
    links.start(dp.at[ys[2], pl.ds(2, 2)], dpa.at[1], d_a + 1, at_y(ys[3]))
    links.arrived(dpa.at[0], d_a, at_y(ys[3]))
    head = pl.ds(0, 2)
    dp[ys[1], head] = (dp[ys[1], head].astype(F32) + dpa[0].astype(F32)).astype(BF16)
    links.start(dp.at[ys[1]], dpb.at[0], d_b, at_y(ys[1]))
    links.arrived(dpa.at[1], d_a + 1, at_y(ys[1]))
    tail = pl.ds(2, 2)
    dp[ys[3], tail] = (dp[ys[3], tail].astype(F32) + dpa[1].astype(F32)).astype(BF16)
    links.start(dp.at[ys[3]], dpb.at[1], d_b + 1, at_y(ys[3]))
    links.arrived(dpb.at[0], d_b, at_y(ys[3]))
    links.arrived(dpb.at[1], d_b + 1, at_y(ys[1]))
    row = lax.broadcasted_iota(jnp.int32, (64, 16), 0)
    col = lax.broadcasted_iota(jnp.int32, (64, 16), 1)
    same = (row // 16 == col // 4) & (lax.rem(row, 4) == lax.rem(col, 4))
    blocks = None
    for p in range(4):
        total = dp[y, p].astype(F32) + dpb[0, p].astype(F32) + dpb[1, p].astype(F32)
        pick = jnp.where(same & (lax.rem(row, 16) // 4 == p), 1.0, 0.0).astype(BF16)
        term = dot_nn(pick, total.astype(BF16))
        blocks = term if blocks is None else blocks + term
    zb[...] = blocks.astype(BF16).reshape(4, 16, 1792)
    d_z = links.new_recv(3)
    for i in (1, 2, 3):
        links.start(zb.at[zs[i]], zr.at[z], d_z + i - 1, at_z(zs[i]))
    zr[z] = zb[z]
    for i in (1, 2, 3):
        links.arrived(zr.at[zs[4 - i]], d_z + i - 1, at_z(zs[4 - i]))

    for p in range(4):
        cols = slice(p * 1792, (p + 1) * 1792)
        value = mixed[:, cols]
        for e in range(2):
            pick = chosen[4 * e + p][:, :16].astype(BF16)
            rows = dot_nn(pick, zr[2 * e]) + dot_nn(pick, zr[2 * e + 1])
            value = value + gates[e] * rows
        out[:, cols] = value.astype(BF16)

    links.finish()
    for own, remote in out_sends:

        @pl.when(jnp.logical_not(own))
        def _():
            remote().wait_send()


def body(
    hidden_in, queries, span_latent, cache_latent, cache_len, value_up, out_proj, norm_gain,
    expert_gate, expert_up, expert_down, routes, route_weights,
):
    c = lax.axis_index("ctx")
    route_row = lax.dynamic_slice_in_dim(routes[0], c * 64, 64, 0)
    weight_row = lax.dynamic_slice_in_dim(route_weights[0], c * 64, 64, 0)
    vmem = pl.BlockSpec(memory_space=pltpu.VMEM)
    hbm = pl.BlockSpec(memory_space=pl.ANY)
    smem = pl.BlockSpec(memory_space=pltpu.SMEM)
    result = pl.pallas_call(
        kernel,
        out_shape=jax.ShapeDtypeStruct((64, 7168), BF16),
        in_specs=[smem, vmem, vmem, vmem, vmem, vmem, vmem, vmem, hbm, hbm, hbm, hbm, hbm],
        out_specs=vmem,
        scratch_shapes=[
            pltpu.VMEM((2, 16, 64, 576), BF16),
            pltpu.VMEM((512, 576), BF16),
            pltpu.VMEM((4, 4, 2, 64, 576), BF16),
            pltpu.VMEM((2, 4, 4, 4, 128, 128), BF16),
            pltpu.VMEM((3, 2, 4, 2, 448, 256), BF16),
            pltpu.VMEM((4, 4, 2, 448, 256), BF16),
            pltpu.VMEM((4, 4, 2, 64, 512), BF16),
            pltpu.VMEM((4, 64, 1024), BF16),
            pltpu.VMEM((4, 2, 64, 1024), BF16),
            pltpu.VMEM((4, 4, 2, 64, 896), BF16),
            pltpu.VMEM((4, 2, 64, 896), BF16),
            pltpu.VMEM((4, 2, 2, 64, 896), BF16),
            pltpu.VMEM((4, 64, 896), BF16),
            pltpu.VMEM((4, 64, 896), BF16),
            pltpu.VMEM((64, 7168), F32),
            pltpu.VMEM((64, 7168), BF16),
            pltpu.VMEM((2, 16, 1792), BF16),
            pltpu.VMEM((4, 16, 1792), BF16),
            pltpu.VMEM((4, 4, 16, 1792), BF16),
            pltpu.VMEM((4, 4, 16, 1792), BF16),
            pltpu.VMEM((2, 2, 16, 1792), BF16),
            pltpu.VMEM((2, 4, 16, 1792), BF16),
            pltpu.VMEM((4, 16, 1792), BF16),
            pltpu.VMEM((4, 16, 1792), BF16),
            pltpu.SemaphoreType.DMA((N_SEND,)),
            pltpu.SemaphoreType.DMA((N_RECV,)),
            pltpu.SemaphoreType.DMA((8,)),
        ],
        compiler_params=pltpu.CompilerParams(
            collective_id=0, has_side_effects=True, vmem_limit_bytes=60 * 1024 * 1024
        ),
        name="layer",
    )(
        cache_len, hidden_in[0], queries[0], span_latent[0], cache_latent[0],
        norm_gain[None], route_row, weight_row,
        value_up, out_proj, expert_gate, expert_up, expert_down,
    )
    return result[None]


def solution(mesh):
    in_specs = (
        P("fsdp", "ctx", None),
        P("fsdp", "ctx", None),
        P("fsdp", "ctx", None),
        P("fsdp", "ctx", None),
        P("fsdp", None),
        P("ctx", None, None),
        P("fsdp", "ctx"),
        P(),
        P("fsdp", "ctx"),
        P("fsdp", "ctx"),
        P("fsdp", "ctx"),
        P("fsdp", None, None),
        P("fsdp", None, None),
    )
    out_specs = P("fsdp", "ctx", None)
    return jax.shard_map(body, mesh=mesh, in_specs=in_specs, out_specs=out_specs, check_vma=False)
```

```python
import functools

import jax
import jax.numpy as jnp
from jax import lax
from jax.experimental import pallas as pl
from jax.experimental.pallas import tpu as pltpu
from jax.sharding import PartitionSpec as P

MESH = pl.DeviceIdType.MESH
F32 = jnp.float32
BF16 = jnp.bfloat16

CAP = 4
SCALE_LOG2 = 192.0 ** (-0.5) * 1.4426950408889634
EPSILON = 1e-06
NEGATIVE = -1e30
N_SEND = 128
N_RECV = 128


def dot_nt(a, b):
    return lax.dot_general(a, b, (((1,), (1,)), ((), ())), preferred_element_type=F32)


def dot_nn(a, b):
    return jnp.dot(a, b, preferred_element_type=F32)


class Links:
    def __init__(self, send, recv):
        self.send, self.recv = send, recv
        self.n_send = self.n_recv = 0
        self.open = []

    def new_recv(self, count=1):
        base = self.n_recv
        self.n_recv += count
        assert self.n_recv <= N_RECV
        return base

    def start(self, src, dst, recv_index, device):
        copy = pltpu.make_async_remote_copy(
            src_ref=src,
            dst_ref=dst,
            send_sem=self.send.at[self.n_send],
            recv_sem=self.recv.at[recv_index],
            device_id=device,
            device_id_type=MESH,
        )
        self.n_send += 1
        assert self.n_send <= N_SEND
        copy.start()
        self.open.append(copy)

    def arrived(self, dst, recv_index, device):
        pltpu.make_async_remote_copy(
            src_ref=dst,
            dst_ref=dst,
            send_sem=self.send.at[0],
            recv_sem=self.recv.at[recv_index],
            device_id=device,
            device_id_type=MESH,
        ).wait_recv()

    def finish(self):
        for copy in self.open:
            copy.wait_send()


class Ring:
    def __init__(self, links, at, device, chunk, half):
        self.links, self.at, self.device = links, at, device
        self.chunk, self.half = chunk, half
        self.base = links.new_recv(4)
        self.up, self.down, self.far = (lax.rem(at + i, 4) for i in (1, 3, 2))

    def start(self):
        own = self.chunk(self.at)
        self.links.start(own, own, self.base, self.device(self.up))
        self.links.start(own, own, self.base + 1, self.device(self.down))

    def forward(self):
        self.links.arrived(self.chunk(self.down), self.base, self.device(self.down))
        part = self.half(self.down, 0)
        self.links.start(part, part, self.base + 2, self.device(self.up))
        self.links.arrived(self.chunk(self.up), self.base + 1, self.device(self.up))
        part = self.half(self.up, 1)
        self.links.start(part, part, self.base + 3, self.device(self.down))

    def finish(self):
        self.links.arrived(self.half(self.far, 0), self.base + 2, self.device(self.down))
        self.links.arrived(self.half(self.far, 1), self.base + 3, self.device(self.up))


def kernel(
    lens, hid_in, q_in, span, cache, gain, routes_in, weights_in,
    vu_in, wo_in, wg_in, wu_in, wd_in,
    out,
    kb, kc, qs, vbuf, wbuf, wo, att, ho, hb,
    part, rsa, rsb, zsend, zrecv, mixed, sel, hs, sp, sq, sx, sy, nrm,
    sb, sblk, yb, dp, dpa, dpb, zb, zr, hid, q, routes, weights,
    send_sems, recv_sems, local_sems,
):
    c, f = lax.axis_index("ctx"), lax.axis_index("fsdp")
    z, y = c // 4, lax.rem(c, 4)
    zh, x, k = f // 8, lax.rem(f // 2, 4), lax.rem(f, 2)
    zm = lax.rem(z, 2)
    place_z = zh * 4 + z
    expert = 1 - z // 2
    links = Links(send_sems, recv_sems)

    def at_z(z2):
        return {"ctx": z2 * 4 + y, "fsdp": f}

    def at_y(y2):
        return {"ctx": z * 4 + y2, "fsdp": f}

    def at_x(x2):
        return {"ctx": c, "fsdp": zh * 8 + x2 * 2 + k}

    def at_zh(z2, zh2):
        return {"ctx": z2 * 4 + y, "fsdp": zh2 * 8 + x * 2 + k}

    other_core = {"ctx": c, "fsdp": zh * 8 + x * 2 + (1 - k)}
    up_two, down_two = lax.rem(place_z + 2, 8), lax.rem(place_z + 6, 8)
    twos = [at_zh(lax.rem(p, 4), p // 4) for p in (up_two, down_two)]
    partner = z + 1 - 2 * zm
    pair = at_z(partner)

    def at_pair(y2):
        return {"ctx": partner * 4 + y2, "fsdp": f}

    zs = [lax.rem(z + i, 4) for i in range(4)]
    ys = [lax.rem(y + i, 4) for i in range(4)]
    xs = [lax.rem(x + i, 4) for i in range(4)]

    local = []

    def place(src, dst):
        copy = pltpu.make_async_copy(src, dst, local_sems.at[len(local)])
        copy.start()
        local.append(copy)

    place(cache, kb.at[0, c])
    place(span, kb.at[1, c])
    place(vu_in.at[k, pl.ds(pl.multiple_of(x * 128, 128), 128)], vbuf.at[k, x, z, y])
    place(q_in, q)
    place(hid_in, hid)
    place(routes_in, routes)
    place(weights_in, weights)

    barrier = pltpu.get_barrier_semaphore()
    peers = [at_y(ys[i]) for i in (1, 2, 3)] + [at_x(xs[i]) for i in (1, 2, 3)] + [other_core]
    peers += [at_zh(zs[i], zh) for i in (1, 2, 3)] + [at_zh(zs[i], 1 - zh) for i in range(4)]
    peers += [at_pair(ys[i]) for i in (1, 2, 3)]
    for peer in peers:
        pl.semaphore_signal(barrier, inc=1, device_id=peer, device_id_type=MESH)
    pl.semaphore_wait(barrier, len(peers))
    for copy in local[:3]:
        copy.wait()

    vu_z = links.new_recv(3)
    for i in (1, 2, 3):
        own = vbuf.at[k, x, z, y]
        links.start(own, own, vu_z + i - 1, at_z(zs[i]))
    keys_z = links.new_recv(3)
    for i in (1, 2, 3):
        links.start(kb.at[:, c], kb.at[:, c], keys_z + i - 1, at_z(zs[i]))
    out_z = links.new_recv(4)
    out_sends = []
    for a in range(2):
        for b in range(2):
            z2 = zh + 2 * a
            own = (z2 == z) & (zh == b)
            sem = links.n_send
            links.n_send += 1

            def remote(sem=sem, z2=z2, b=b):
                return pltpu.make_async_remote_copy(
                    src_ref=wo_in,
                    dst_ref=wo.at[z, x, k],
                    send_sem=send_sems.at[sem],
                    recv_sem=recv_sems.at[out_z + z],
                    device_id=at_zh(z2, b),
                    device_id_type=MESH,
                )

            @pl.when(own)
            def _():
                pltpu.make_async_copy(wo_in, wo.at[z, x, k], recv_sems.at[out_z + z]).start()

            @pl.when(jnp.logical_not(own))
            def _():
                remote().start()

            out_sends.append((own, remote))

    keys_y = []
    for i in range(4):
        zi = zs[i]
        keys_y.append(
            Ring(
                links, y, at_y,
                lambda o, zi=zi: kb.at[:, zi * 4 + o],
                lambda o, j, zi=zi: kb.at[j, zi * 4 + o],
            )
        )
    keys_y[0].start()
    vu_y = Ring(
        links, y, at_y,
        lambda o: vbuf.at[k, x, :, o],
        lambda o, j: vbuf.at[k, x, pl.ds(2 * j, 2), o],
    )
    vu_x = Ring(
        links, x, at_x,
        lambda o: vbuf.at[k, o],
        lambda o, j: vbuf.at[k, o, pl.ds(2 * j, 2)],
    )
    gu_x = Ring(
        links, x, at_x,
        lambda o: wbuf.at[pl.ds(0, 2), :, o, k],
        lambda o, j: wbuf.at[pl.ds(0, 2), j, o, k],
    )
    down_x = Ring(
        links, x, at_x,
        lambda o: wbuf.at[2, :, o, k],
        lambda o, j: wbuf.at[2, j, o, k],
    )
    out_x = Ring(
        links, x, at_x,
        lambda o: wo.at[:, o, k],
        lambda o, j: wo.at[pl.ds(2 * j, 2), o, k],
    )
    expert_z = links.new_recv(6)

    def send_expert(w, ref):
        for p in twos:
            links.start(ref, wbuf.at[w, zh, x, k], expert_z + 2 * w + zh, p)

    def got_expert(w):
        for h in range(2):
            links.arrived(wbuf.at[w, h, x, k], expert_z + 2 * w + h, twos[0])

    def relayout(index, carry):
        zq, yq = index // 4, lax.rem(index, 4)
        cols = q[:, pl.ds(pl.multiple_of(index * 1152, 128), 1152)]
        qs[yq, zq, 0] = cols[:, :576]
        qs[yq, zq, 1] = cols[:, 576:]
        return carry

    for i in (1, 2, 3):
        links.arrived(vbuf.at[k, x, zs[4 - i], y], vu_z + i - 1, at_z(zs[4 - i]))
    vu_y.start()
    local[3].wait()
    lax.fori_loop(0, 16, relayout, 0)
    vu_y.forward()

    for copy in local[4:]:
        copy.wait()
    near = pl.ds(pl.multiple_of((c // 2) * 128, 128), 128)

    def own_tokens(ref):
        both = ref[:, near]
        return jnp.where(lax.rem(c, 2) == 1, both[:, 64:], both[:, :64])

    own_routes, own_weights = own_tokens(routes), own_tokens(weights)
    earlier = lax.broadcasted_iota(jnp.int32, (64, 64), 0) < lax.broadcasted_iota(
        jnp.int32, (64, 64), 1
    )
    earlier = jnp.where(earlier, 1.0, 0.0).astype(BF16)
    slot_row = lax.broadcasted_iota(jnp.int32, (128, 64), 0)
    chosen, gates, mine = [], [], []
    for e in range(2):
        match = own_routes == e
        hit = jnp.sum(jnp.where(match, 1.0, 0.0), axis=0, keepdims=True)
        weight = jnp.sum(jnp.where(match, own_weights, 0.0), axis=0, keepdims=True)
        within = dot_nn(jnp.broadcast_to(hit, (16, 64)).astype(BF16), earlier)[:1]
        named = (hit > 0.5) & (within.astype(jnp.int32) == lax.rem(slot_row, 4))
        mine.append((hit, within))
        for p in range(4):
            chosen.append(jnp.where(named & (slot_row // 4 == p), 1.0, 0.0))
        gates.append(
            jnp.sum(jnp.where(named & (slot_row < 16), weight, 0.0)[:16], axis=1, keepdims=True)
        )

    pair_routes = routes[:, pl.ds(pl.multiple_of((z // 2) * 512, 128), 512)]
    row = lax.broadcasted_iota(jnp.int32, (128, 128), 0)
    col = lax.broadcasted_iota(jnp.int32, (128, 128), 1)
    earlier = jnp.where((row < col) & (row // 64 == col // 64), 1.0, 0.0).astype(BF16)
    hits, places = [], []
    for e in range(2):
        hit = jnp.sum(jnp.where(pair_routes == e, 1.0, 0.0), axis=0, keepdims=True)
        wide = jnp.broadcast_to(hit, (16, 512)).astype(BF16)
        counts = [dot_nn(wide[:, i * 128 : (i + 1) * 128], earlier)[:1] for i in range(4)]
        hits.append(hit)
        places.append(jnp.concatenate(counts, axis=1))
    row = lax.broadcasted_iota(jnp.int32, (64, 512), 0)
    col = lax.broadcasted_iota(jnp.int32, (64, 512), 1)
    first = lax.rem(row // 4, 2) == 0
    hit = jnp.where(first, hits[0], hits[1])
    place_of = jnp.where(first, places[0], places[1]).astype(jnp.int32)
    here = (row // 16 == lax.rem(col // 64, 4)) & (lax.rem(row // 8, 2) == col // 256)
    pick = here & (hit > 0.5) & (place_of == lax.rem(row, 4))
    sel[...] = jnp.where(pick, 1.0, 0.0).astype(BF16)
    row = lax.broadcasted_iota(jnp.int32, (16, 64), 0)
    first = lax.rem(row // 4, 2) == 0
    hit = jnp.where(first, mine[0][0], mine[1][0])
    place_of = jnp.where(first, mine[0][1], mine[1][1]).astype(jnp.int32)
    pick = (row // 8 == zm) & (hit > 0.5) & (place_of == lax.rem(row, 4))
    own_slots = jnp.where(pick, 1.0, 0.0).astype(BF16)


    def key_block(i):
        links.arrived(kb.at[:, zs[4 - i] * 4 + y], keys_z + i - 1, at_z(zs[4 - i]))
        keys_y[4 - i].start()

    key_block(1)
    keys_y[0].forward()
    vu_y.finish()
    vu_x.start()
    key_block(2)
    keys_y[3].forward()
    key_block(3)

    keys_y[2].forward()
    keys_y[1].forward()
    vu_x.forward()
    vu_core = links.new_recv(1)
    out_core = links.new_recv(4)
    gu_core, down_core = links.new_recv(1), links.new_recv(1)
    for i in range(4):
        links.arrived(wo.at[i, x, k], out_z + i, at_z(zs[1]))
    out_x.start()
    links.start(wo.at[:, x, k], wo.at[:, x, k], out_core, other_core)
    send_expert(0, wg_in)
    send_expert(1, wu_in)
    for i in (0, 3, 2, 1):
        keys_y[i].finish()

    slot = lax.broadcasted_iota(jnp.int32, (512, 128), 0)
    lane = lax.broadcasted_iota(jnp.int32, (512, 128), 1)
    packed = None
    first = 0
    for b in range(0, 16, 2):
        len0, len1 = lens[0, b], lens[0, b + 1]
        left = (lane < len0) & (slot == lane + first)
        right = (lane >= 64) & (lane < 64 + len1) & (slot == lane - 64 + (first + len0))
        pick = jnp.where(left & (lane < 64) | right, 1.0, 0.0).astype(BF16)
        term = dot_nn(pick, kb[0, pl.ds(b, 2)].reshape(128, 576))
        packed = term if packed is None else packed + term
        first = first + len0 + len1
    kc[...] = packed.astype(BF16)

    def attend(group):
        def step(half, carry):
            rows = qs[group, pl.ds(2 * half, 2)].reshape(256, 576)
            s1 = dot_nt(rows, kc[...])
            s2 = dot_nt(rows, kb[1].reshape(1024, 576))
            token = lax.rem(lax.broadcasted_iota(jnp.int32, (256, 1024), 0), 64)
            key = lax.broadcasted_iota(jnp.int32, (256, 1024), 1)
            s2 = jnp.where(key <= token + c * 64, s2, NEGATIVE)
            top = jnp.maximum(
                jnp.max(s1, axis=1, keepdims=True), jnp.max(s2, axis=1, keepdims=True)
            )
            p1 = jnp.exp2((s1 - top) * SCALE_LOG2)
            p2 = jnp.exp2((s2 - top) * SCALE_LOG2)
            total = jnp.sum(p1, axis=1, keepdims=True) + jnp.sum(p2, axis=1, keepdims=True)
            acc = dot_nn(p1.astype(BF16), kc[:, :512])
            acc = acc + dot_nn(p2.astype(BF16), kb[1, :, :, :512].reshape(1024, 512))
            att[group, pl.ds(2 * half, 2)] = (acc / total).astype(BF16).reshape(2, 2, 64, 512)
            return carry

        lax.fori_loop(0, 2, step, 0)

    ho_y, ho_z = links.new_recv(4), links.new_recv(4)

    def head_outputs(i):
        group = ys[i]
        for zq in range(4):
            pieces = []
            for j in range(2):
                value = jnp.concatenate([vbuf[j, r, zq, group] for r in range(4)], axis=0)
                pieces.append(dot_nn(att[group, zq, j], value).astype(BF16))
            ho[i, :, zq * 256 : (zq + 1) * 256] = jnp.concatenate(pieces, axis=1)
        links.start(ho.at[i], hb.at[zm, y], ho_z + i, at_pair(group))
        if i:
            links.start(ho.at[i], hb.at[zm, y], ho_y + i, at_y(group))
        else:
            hb[zm, y] = ho[0]

    vu_x.finish()
    links.start(vbuf.at[k], vbuf.at[k], vu_core, other_core)
    attend(ys[2])
    attend(ys[1])
    links.arrived(vbuf.at[1 - k], vu_core, other_core)
    head_outputs(2)
    head_outputs(1)
    attend(ys[3])
    head_outputs(3)
    attend(ys[0])
    head_outputs(0)
    out_x.forward()
    for i in (1, 3):
        links.start(wo.at[:, xs[i], k], wo.at[:, xs[i], k], out_core + i, other_core)
    got_expert(0)
    got_expert(1)

    rs_a, rs_b, rs_z = links.new_recv(8), links.new_recv(8), links.new_recv(4)
    tiles = (0, 1, 3, 2)

    def project(n):
        i = tiles[n]
        acc = None
        for zq in range(4):
            term = dot_nt(
                hb[:, :, :, zq * 256 : (zq + 1) * 256].reshape(512, 256),
                wo[zq, xs[i]].reshape(896, 256),
            )
            acc = term if acc is None else acc + term
        part[n] = acc.astype(BF16).reshape(2, 4, 64, 896)
        links.start(part.at[n, 0, ys[2]], rsa.at[n, 0], rs_a + 2 * n, at_y(ys[1]))
        links.start(part.at[n, 1, ys[2]], rsa.at[n, 1], rs_a + 2 * n + 1, at_y(ys[3]))

    def pass_on(n):
        links.arrived(rsa.at[n, 0], rs_a + 2 * n, at_y(ys[3]))
        part[n, 0, ys[1]] = (part[n, 0, ys[1]].astype(F32) + rsa[n, 0].astype(F32)).astype(BF16)
        links.start(part.at[n, :, ys[1]], rsb.at[n, 0], rs_b + 2 * n, at_y(ys[1]))
        links.arrived(rsa.at[n, 1], rs_a + 2 * n + 1, at_y(ys[1]))
        part[n, 1, ys[3]] = (part[n, 1, ys[3]].astype(F32) + rsa[n, 1].astype(F32)).astype(BF16)
        links.start(part.at[n, :, ys[3]], rsb.at[n, 1], rs_b + 2 * n + 1, at_y(ys[3]))

    def columns(half, n):
        return pl.ds(pl.multiple_of(half * 3584 + xs[tiles[n]] * 896, 128), 896)

    def collect(n):
        links.arrived(rsb.at[n, 0], rs_b + 2 * n, at_y(ys[3]))
        links.arrived(rsb.at[n, 1], rs_b + 2 * n + 1, at_y(ys[1]))

        def total(member):
            return (
                part[n, member, y].astype(F32)
                + rsb[n, 0, member].astype(F32)
                + rsb[n, 1, member].astype(F32)
            )

        zsend[n] = total(1 - zm).astype(BF16)
        links.start(zsend.at[n], zrecv.at[n], rs_z + n, pair)
        cols = columns(zm, n)
        mixed[:, cols] = hid[:, cols].astype(F32) + total(zm)

    def slot_tile(n):
        i = tiles[n]
        links.arrived(wo.at[:, xs[i], 1 - k], out_core + i, other_core)
        acc = None
        for zq in range(4):
            term = dot_nt(hs[:, zq * 256 : (zq + 1) * 256], wo[zq, xs[i]].reshape(896, 256))
            acc = term if acc is None else acc + term
        sp[:, xs[i]] = acc.astype(BF16).reshape(4, 16, 896)

    for i in (2, 1, 3, 0):
        source = ys[(4 - i) % 4]
        if i:
            links.arrived(hb.at[zm, source], ho_y + i, at_y(source))
        links.arrived(hb.at[1 - zm, source], ho_z + i, at_pair(source))
    hs[...] = dot_nn(sel[...], hb[...].reshape(512, 1024)).astype(BF16)
    slot_tile(0)
    project(0)
    slot_tile(1)
    slot_tile(2)
    out_x.finish()
    links.start(wo.at[:, xs[2], k], wo.at[:, xs[2], k], out_core + 2, other_core)
    gu_x.start()
    send_expert(2, wd_in)
    slot_tile(3)
    slot_y, slot_z = links.new_recv(3), links.new_recv(1)
    for i in (1, 2, 3):
        links.start(sp.at[ys[i]], sq.at[i - 1], slot_y + i - 1, at_y(ys[i]))
    project(1)
    for i in (1, 2, 3):
        links.arrived(sq.at[i - 1], slot_y + i - 1, at_y(ys[4 - i]))
    half = sp[y].astype(F32) + sq[0].astype(F32) + sq[1].astype(F32) + sq[2].astype(F32)
    sx[...] = half.astype(BF16)
    links.start(sx, sy, slot_z, pair)
    nrm[zm] = half
    pass_on(0)
    project(2)
    links.arrived(sy, slot_z, pair)
    nrm[1 - zm] = sy[...].astype(F32)
    square = None
    for r in range(8):
        cols = slice(r * 896, (r + 1) * 896)
        block = nrm[r // 4, r % 4] + dot_nn(own_slots, hid[:, cols])
        nrm[r // 4, r % 4] = block
        term = jnp.sum(block * block, axis=1, keepdims=True)
        square = term if square is None else square + term
    inverse = lax.rsqrt(square * (1.0 / 7168.0) + EPSILON)
    row = lax.broadcasted_iota(jnp.int32, (16, 16), 0)
    col = lax.broadcasted_iota(jnp.int32, (16, 16), 1)
    blocks = [None, None]
    for p in range(4):
        pieces = []
        for r in (2 * p, 2 * p + 1):
            cols = slice(r * 896, (r + 1) * 896)
            pieces.append((nrm[r // 4, r % 4] * inverse * gain[:, cols]).astype(BF16))
        rows = jnp.concatenate(pieces, axis=1)
        for e in range(2):
            pick = (row // 4 == p) & (col == zm * 8 + e * 4 + lax.rem(row, 4))
            term = dot_nn(jnp.where(pick, 1.0, 0.0).astype(BF16), rows)
            blocks[e] = term if blocks[e] is None else blocks[e] + term
    for e in range(2):
        sb[e] = blocks[e].astype(BF16)
    sl_z = links.new_recv(3)
    for i in (1, 2, 3):
        links.start(sb.at[1 - zs[i] // 2], sblk.at[z], sl_z + i - 1, at_z(zs[i]))
    sblk[z] = sb[expert]
    pass_on(1)
    collect(0)
    project(3)
    for i in (1, 2, 3):
        links.arrived(sblk.at[zs[4 - i]], sl_z + i - 1, at_z(zs[4 - i]))
    stacked = sblk[...].reshape(64, 1792)
    row = lax.broadcasted_iota(jnp.int32, (16, 64), 0)
    col = lax.broadcasted_iota(jnp.int32, (16, 64), 1)
    same = (row // 4 == col // 16) & (lax.rem(row, 4) == lax.rem(col, 4))
    for p in range(4):
        pick = jnp.where(same & (lax.rem(col, 16) // 4 == p), 1.0, 0.0).astype(BF16)
        yb[y, p] = dot_nn(pick, stacked).astype(BF16)
    sl_y = Ring(
        links, y, at_y,
        lambda o: yb.at[o],
        lambda o, j: yb.at[o, pl.ds(2 * j, 2)],
    )
    sl_y.start()
    gu_x.forward()
    got_expert(2)
    down_x.start()
    pass_on(2)
    sl_y.forward()
    collect(1)
    pass_on(3)
    gu_x.finish()
    ready = wbuf.at[pl.ds(0, 2), :, :, k]
    links.start(ready, ready, gu_core, other_core)
    sl_y.finish()
    down_x.forward()
    links.arrived(wbuf.at[pl.ds(0, 2), :, :, 1 - k], gu_core, other_core)

    gate_acc = up_acc = None
    for p in range(4):
        rows = yb[:, p].reshape(64, 1792)
        span_x = pl.ds(2 * (p % 2), 2)
        g_term = dot_nn(rows, wbuf[0, p // 2, span_x].reshape(1792, 256))
        u_term = dot_nn(rows, wbuf[1, p // 2, span_x].reshape(1792, 256))
        gate_acc = g_term if gate_acc is None else gate_acc + g_term
        up_acc = u_term if up_acc is None else up_acc + u_term
    down_x.finish()
    links.start(wbuf.at[2, :, :, k], wbuf.at[2, :, :, k], down_core, other_core)
    act = (gate_acc / (1.0 + jnp.exp(-gate_acc)) * up_acc).astype(BF16)
    links.arrived(wbuf.at[2, :, :, 1 - k], down_core, other_core)
    for p in range(4):
        down = dot_nt(act, wbuf[2, p // 2, pl.ds(2 * (p % 2), 2)].reshape(1792, 256))
        dp[:, p] = down.astype(BF16).reshape(4, 16, 1792)

    collect(2)
    collect(3)
    d_a, d_b = links.new_recv(2), links.new_recv(2)
    links.start(dp.at[ys[2], pl.ds(0, 2)], dpa.at[0], d_a, at_y(ys[1]))
    links.start(dp.at[ys[2], pl.ds(2, 2)], dpa.at[1], d_a + 1, at_y(ys[3]))
    links.arrived(dpa.at[0], d_a, at_y(ys[3]))
    head = pl.ds(0, 2)
    dp[ys[1], head] = (dp[ys[1], head].astype(F32) + dpa[0].astype(F32)).astype(BF16)
    links.start(dp.at[ys[1]], dpb.at[0], d_b, at_y(ys[1]))
    links.arrived(dpa.at[1], d_a + 1, at_y(ys[1]))
    tail = pl.ds(2, 2)
    dp[ys[3], tail] = (dp[ys[3], tail].astype(F32) + dpa[1].astype(F32)).astype(BF16)
    links.start(dp.at[ys[3]], dpb.at[1], d_b + 1, at_y(ys[3]))
    links.arrived(dpb.at[0], d_b, at_y(ys[3]))
    links.arrived(dpb.at[1], d_b + 1, at_y(ys[1]))
    row = lax.broadcasted_iota(jnp.int32, (64, 16), 0)
    col = lax.broadcasted_iota(jnp.int32, (64, 16), 1)
    same = (row // 16 == col // 4) & (lax.rem(row, 4) == lax.rem(col, 4))
    blocks = None
    for p in range(4):
        total = dp[y, p].astype(F32) + dpb[0, p].astype(F32) + dpb[1, p].astype(F32)
        pick = jnp.where(same & (lax.rem(row, 16) // 4 == p), 1.0, 0.0).astype(BF16)
        term = dot_nn(pick, total.astype(BF16))
        blocks = term if blocks is None else blocks + term
    zb[...] = blocks.astype(BF16).reshape(4, 16, 1792)
    d_z = links.new_recv(3)
    for i in (1, 2, 3):
        links.start(zb.at[zs[i]], zr.at[z], d_z + i - 1, at_z(zs[i]))
    zr[z] = zb[z]
    for n in range(4):
        links.arrived(zrecv.at[n], rs_z + n, pair)
        cols = columns(1 - zm, n)
        mixed[:, cols] = hid[:, cols].astype(F32) + zrecv[n].astype(F32)
    for i in (1, 2, 3):
        links.arrived(zr.at[zs[4 - i]], d_z + i - 1, at_z(zs[4 - i]))

    for e in range(2):
        rows = zr[2 - 2 * e].astype(F32) + zr[3 - 2 * e].astype(F32)
        sblk[e] = (rows * gates[e]).astype(BF16)
    for p in range(4):
        cols = slice(p * 1792, (p + 1) * 1792)
        value = mixed[:, cols]
        for e in range(2):
            pick = jnp.transpose(chosen[4 * e + p])[:, :16].astype(BF16)
            value = value + dot_nn(pick, sblk[e])
        out[:, cols] = value.astype(BF16)

    links.finish()
    for own, remote in out_sends:

        @pl.when(jnp.logical_not(own))
        def _():
            remote().wait_send()


def body(
    hidden_in, queries, span_latent, cache_latent, cache_len, value_up, out_proj, norm_gain,
    expert_gate, expert_up, expert_down, routes, route_weights,
):
    vmem = pl.BlockSpec(memory_space=pltpu.VMEM)
    hbm = pl.BlockSpec(memory_space=pl.ANY)
    smem = pl.BlockSpec(memory_space=pltpu.SMEM)
    result = pl.pallas_call(
        kernel,
        out_shape=jax.ShapeDtypeStruct((64, 7168), BF16),
        in_specs=[smem, hbm, hbm, hbm, hbm, vmem, hbm, hbm, hbm, hbm, hbm, hbm, hbm],
        out_specs=vmem,
        scratch_shapes=[
            pltpu.VMEM((2, 16, 64, 576), BF16),
            pltpu.VMEM((512, 576), BF16),
            pltpu.VMEM((4, 4, 2, 64, 576), BF16),
            pltpu.VMEM((2, 4, 4, 4, 128, 128), BF16),
            pltpu.VMEM((3, 2, 4, 2, 448, 256), BF16),
            pltpu.VMEM((4, 4, 2, 448, 256), BF16),
            pltpu.VMEM((4, 4, 2, 64, 512), BF16),
            pltpu.VMEM((4, 64, 1024), BF16),
            pltpu.VMEM((2, 4, 64, 1024), BF16),
            pltpu.VMEM((4, 2, 4, 64, 896), BF16),
            pltpu.VMEM((4, 2, 64, 896), BF16),
            pltpu.VMEM((4, 2, 2, 64, 896), BF16),
            pltpu.VMEM((4, 64, 896), BF16),
            pltpu.VMEM((4, 64, 896), BF16),
            pltpu.VMEM((64, 7168), F32),
            pltpu.VMEM((64, 512), BF16),
            pltpu.VMEM((64, 1024), BF16),
            pltpu.VMEM((4, 4, 16, 896), BF16),
            pltpu.VMEM((3, 4, 16, 896), BF16),
            pltpu.VMEM((4, 16, 896), BF16),
            pltpu.VMEM((4, 16, 896), BF16),
            pltpu.VMEM((2, 4, 16, 896), F32),
            pltpu.VMEM((2, 16, 1792), BF16),
            pltpu.VMEM((4, 16, 1792), BF16),
            pltpu.VMEM((4, 4, 16, 1792), BF16),
            pltpu.VMEM((4, 4, 16, 1792), BF16),
            pltpu.VMEM((2, 2, 16, 1792), BF16),
            pltpu.VMEM((2, 4, 16, 1792), BF16),
            pltpu.VMEM((4, 16, 1792), BF16),
            pltpu.VMEM((4, 16, 1792), BF16),
            pltpu.VMEM((64, 7168), BF16),
            pltpu.VMEM((64, 18432), BF16),
            pltpu.VMEM((8, 1024), jnp.int32),
            pltpu.VMEM((8, 1024), F32),
            pltpu.SemaphoreType.DMA((N_SEND,)),
            pltpu.SemaphoreType.DMA((N_RECV,)),
            pltpu.SemaphoreType.DMA((8,)),
        ],
        compiler_params=pltpu.CompilerParams(
            collective_id=0, has_side_effects=True, vmem_limit_bytes=60 * 1024 * 1024
        ),
        name="layer",
    )(
        cache_len, hidden_in[0], queries[0], span_latent[0], cache_latent[0],
        norm_gain[None], routes[0].T, route_weights[0].T,
        value_up, out_proj, expert_gate, expert_up, expert_down,
    )
    return result[None]


def solution(mesh):
    in_specs = (
        P("fsdp", "ctx", None),
        P("fsdp", "ctx", None),
        P("fsdp", "ctx", None),
        P("fsdp", "ctx", None),
        P("fsdp", None),
        P("ctx", None, None),
        P("fsdp", "ctx"),
        P(),
        P("fsdp", "ctx"),
        P("fsdp", "ctx"),
        P("fsdp", "ctx"),
        P("fsdp", None, None),
        P("fsdp", None, None),
    )
    out_specs = P("fsdp", "ctx", None)
    return jax.shard_map(body, mesh=mesh, in_specs=in_specs, out_specs=out_specs, check_vma=False)
```

```python
import functools

import jax
import jax.numpy as jnp
from jax import lax
from jax.experimental import pallas as pl
from jax.experimental.pallas import tpu as pltpu
from jax.sharding import PartitionSpec as P

MESH = pl.DeviceIdType.MESH
F32 = jnp.float32
BF16 = jnp.bfloat16

CAP = 4
SCALE_LOG2 = 192.0 ** (-0.5) * 1.4426950408889634
EPSILON = 1e-06
NEGATIVE = -1e30
N_SEND = 128
N_RECV = 128


def dot_nt(a, b):
    return lax.dot_general(a, b, (((1,), (1,)), ((), ())), preferred_element_type=F32)


def dot_nn(a, b):
    return jnp.dot(a, b, preferred_element_type=F32)


class Links:
    def __init__(self, send, recv):
        self.send, self.recv = send, recv
        self.n_send = self.n_recv = 0
        self.open = []

    def new_recv(self, count=1):
        base = self.n_recv
        self.n_recv += count
        assert self.n_recv <= N_RECV
        return base

    def start(self, src, dst, recv_index, device):
        copy = pltpu.make_async_remote_copy(
            src_ref=src,
            dst_ref=dst,
            send_sem=self.send.at[self.n_send],
            recv_sem=self.recv.at[recv_index],
            device_id=device,
            device_id_type=MESH,
        )
        self.n_send += 1
        assert self.n_send <= N_SEND
        copy.start()
        self.open.append(copy)

    def arrived(self, dst, recv_index, device):
        pltpu.make_async_remote_copy(
            src_ref=dst,
            dst_ref=dst,
            send_sem=self.send.at[0],
            recv_sem=self.recv.at[recv_index],
            device_id=device,
            device_id_type=MESH,
        ).wait_recv()

    def finish(self):
        for copy in self.open:
            copy.wait_send()


class Ring:
    def __init__(self, links, at, device, chunk, half):
        self.links, self.at, self.device = links, at, device
        self.chunk, self.half = chunk, half
        self.base = links.new_recv(4)
        self.up, self.down, self.far = (lax.rem(at + i, 4) for i in (1, 3, 2))

    def start(self):
        own = self.chunk(self.at)
        self.links.start(own, own, self.base, self.device(self.up))
        self.links.start(own, own, self.base + 1, self.device(self.down))

    def forward(self):
        self.links.arrived(self.chunk(self.down), self.base, self.device(self.down))
        part = self.half(self.down, 0)
        self.links.start(part, part, self.base + 2, self.device(self.up))
        self.links.arrived(self.chunk(self.up), self.base + 1, self.device(self.up))
        part = self.half(self.up, 1)
        self.links.start(part, part, self.base + 3, self.device(self.down))

    def finish(self):
        self.links.arrived(self.half(self.far, 0), self.base + 2, self.device(self.down))
        self.links.arrived(self.half(self.far, 1), self.base + 3, self.device(self.up))


def kernel(
    lens, hid_in, q_in, span, cache, gain, routes_in, weights_in,
    vu_in, wo_in, wg_in, wu_in, wd_in,
    out,
    kb, kc, qs, vbuf, wbuf, wo, att, ho, hb,
    part, rsa, rsb, zsend, zrecv, mixed, sel, hs, sp, sq, sx, sy, nrm,
    sb, sblk, yb, dp, dpa, dpb, zb, zr, hid, q, routes, weights,
    send_sems, recv_sems, local_sems,
):
    c, f = lax.axis_index("ctx"), lax.axis_index("fsdp")
    z, y = c // 4, lax.rem(c, 4)
    zh, x, k = f // 8, lax.rem(f // 2, 4), lax.rem(f, 2)
    zm = lax.rem(z, 2)
    place_z = zh * 4 + z
    expert = 1 - z // 2
    links = Links(send_sems, recv_sems)

    def at_z(z2):
        return {"ctx": z2 * 4 + y, "fsdp": f}

    def at_y(y2):
        return {"ctx": z * 4 + y2, "fsdp": f}

    def at_x(x2):
        return {"ctx": c, "fsdp": zh * 8 + x2 * 2 + k}

    def at_zh(z2, zh2):
        return {"ctx": z2 * 4 + y, "fsdp": zh2 * 8 + x * 2 + k}

    other_core = {"ctx": c, "fsdp": zh * 8 + x * 2 + (1 - k)}
    up_two, down_two = lax.rem(place_z + 2, 8), lax.rem(place_z + 6, 8)
    twos = [at_zh(lax.rem(p, 4), p // 4) for p in (up_two, down_two)]
    partner = z + 1 - 2 * zm
    pair = at_z(partner)

    def at_pair(y2):
        return {"ctx": partner * 4 + y2, "fsdp": f}

    zs = [lax.rem(z + i, 4) for i in range(4)]
    ys = [lax.rem(y + i, 4) for i in range(4)]
    xs = [lax.rem(x + i, 4) for i in range(4)]

    local = []

    def place(src, dst):
        copy = pltpu.make_async_copy(src, dst, local_sems.at[len(local)])
        copy.start()
        local.append(copy)

    place(cache, kb.at[0, c])
    place(span, kb.at[1, c])
    place(vu_in.at[k, pl.ds(pl.multiple_of(x * 128, 128), 128)], vbuf.at[k, x, z, y])
    place(q_in, q)
    place(hid_in, hid)
    place(routes_in, routes)
    place(weights_in, weights)

    barrier = pltpu.get_barrier_semaphore()
    peers = [at_y(ys[i]) for i in (1, 2, 3)] + [at_x(xs[i]) for i in (1, 2, 3)] + [other_core]
    peers += [at_zh(zs[i], zh) for i in (1, 2, 3)] + [at_zh(zs[i], 1 - zh) for i in range(4)]
    peers += [at_pair(ys[i]) for i in (1, 2, 3)]
    for peer in peers:
        pl.semaphore_signal(barrier, inc=1, device_id=peer, device_id_type=MESH)
    pl.semaphore_wait(barrier, len(peers))
    for copy in local[:3]:
        copy.wait()

    vu_z = links.new_recv(3)
    for i in (1, 2, 3):
        own = vbuf.at[k, x, z, y]
        links.start(own, own, vu_z + i - 1, at_z(zs[i]))
    keys_z = links.new_recv(3)
    for i in (1, 2, 3):
        links.start(kb.at[:, c], kb.at[:, c], keys_z + i - 1, at_z(zs[i]))
    out_z = links.new_recv(4)
    out_sends = []
    for a in range(2):
        for b in range(2):
            z2 = zh + 2 * a
            own = (z2 == z) & (zh == b)
            sem = links.n_send
            links.n_send += 1

            def remote(sem=sem, z2=z2, b=b):
                return pltpu.make_async_remote_copy(
                    src_ref=wo_in,
                    dst_ref=wo.at[z, x, k],
                    send_sem=send_sems.at[sem],
                    recv_sem=recv_sems.at[out_z + z],
                    device_id=at_zh(z2, b),
                    device_id_type=MESH,
                )

            @pl.when(own)
            def _():
                pltpu.make_async_copy(wo_in, wo.at[z, x, k], recv_sems.at[out_z + z]).start()

            @pl.when(jnp.logical_not(own))
            def _():
                remote().start()

            out_sends.append((own, remote))

    keys_y = []
    for i in range(4):
        zi = zs[i]
        keys_y.append(
            Ring(
                links, y, at_y,
                lambda o, zi=zi: kb.at[:, zi * 4 + o],
                lambda o, j, zi=zi: kb.at[j, zi * 4 + o],
            )
        )
    keys_y[0].start()
    vu_y = Ring(
        links, y, at_y,
        lambda o: vbuf.at[k, x, :, o],
        lambda o, j: vbuf.at[k, x, pl.ds(2 * j, 2), o],
    )
    vu_x = Ring(
        links, x, at_x,
        lambda o: vbuf.at[k, o],
        lambda o, j: vbuf.at[k, o, pl.ds(2 * j, 2)],
    )
    gu_x = Ring(
        links, x, at_x,
        lambda o: wbuf.at[pl.ds(0, 2), :, o, k],
        lambda o, j: wbuf.at[pl.ds(0, 2), j, o, k],
    )
    down_x = Ring(
        links, x, at_x,
        lambda o: wbuf.at[2, :, o, k],
        lambda o, j: wbuf.at[2, j, o, k],
    )
    out_x = Ring(
        links, x, at_x,
        lambda o: wo.at[:, o, k],
        lambda o, j: wo.at[pl.ds(2 * j, 2), o, k],
    )
    expert_z = links.new_recv(6)

    def send_expert(w, ref):
        for p in twos:
            links.start(ref, wbuf.at[w, zh, x, k], expert_z + 2 * w + zh, p)

    def got_expert(w):
        for h in range(2):
            links.arrived(wbuf.at[w, h, x, k], expert_z + 2 * w + h, twos[0])

    def relayout(index, carry):
        zq, yq = index // 4, lax.rem(index, 4)
        cols = q[:, pl.ds(pl.multiple_of(index * 1152, 128), 1152)]
        qs[yq, zq, 0] = cols[:, :576]
        qs[yq, zq, 1] = cols[:, 576:]
        return carry

    for i in (1, 2, 3):
        links.arrived(vbuf.at[k, x, zs[4 - i], y], vu_z + i - 1, at_z(zs[4 - i]))
    vu_y.start()
    local[3].wait()
    lax.fori_loop(0, 16, relayout, 0)
    vu_y.forward()

    for copy in local[4:]:
        copy.wait()
    near = pl.ds(pl.multiple_of((c // 2) * 128, 128), 128)

    def own_tokens(ref):
        both = ref[:, near]
        return jnp.where(lax.rem(c, 2) == 1, both[:, 64:], both[:, :64])

    own_routes, own_weights = own_tokens(routes), own_tokens(weights)
    earlier = lax.broadcasted_iota(jnp.int32, (64, 64), 0) < lax.broadcasted_iota(
        jnp.int32, (64, 64), 1
    )
    earlier = jnp.where(earlier, 1.0, 0.0).astype(BF16)
    slot_row = lax.broadcasted_iota(jnp.int32, (128, 64), 0)
    chosen, gates, mine = [], [], []
    for e in range(2):
        match = own_routes == e
        hit = jnp.sum(jnp.where(match, 1.0, 0.0), axis=0, keepdims=True)
        weight = jnp.sum(jnp.where(match, own_weights, 0.0), axis=0, keepdims=True)
        within = dot_nn(jnp.broadcast_to(hit, (16, 64)).astype(BF16), earlier)[:1]
        named = (hit > 0.5) & (within.astype(jnp.int32) == lax.rem(slot_row, 4))
        mine.append((hit, within))
        for p in range(4):
            chosen.append(jnp.where(named & (slot_row // 4 == p), 1.0, 0.0))
        gates.append(
            jnp.sum(jnp.where(named & (slot_row < 16), weight, 0.0)[:16], axis=1, keepdims=True)
        )

    pair_routes = routes[:, pl.ds(pl.multiple_of((z // 2) * 512, 128), 512)]
    row = lax.broadcasted_iota(jnp.int32, (128, 128), 0)
    col = lax.broadcasted_iota(jnp.int32, (128, 128), 1)
    earlier = jnp.where((row < col) & (row // 64 == col // 64), 1.0, 0.0).astype(BF16)
    hits, places = [], []
    for e in range(2):
        hit = jnp.sum(jnp.where(pair_routes == e, 1.0, 0.0), axis=0, keepdims=True)
        wide = jnp.broadcast_to(hit, (16, 512)).astype(BF16)
        counts = [dot_nn(wide[:, i * 128 : (i + 1) * 128], earlier)[:1] for i in range(4)]
        hits.append(hit)
        places.append(jnp.concatenate(counts, axis=1))
    row = lax.broadcasted_iota(jnp.int32, (64, 512), 0)
    col = lax.broadcasted_iota(jnp.int32, (64, 512), 1)
    first = lax.rem(row // 4, 2) == 0
    hit = jnp.where(first, hits[0], hits[1])
    place_of = jnp.where(first, places[0], places[1]).astype(jnp.int32)
    here = (row // 16 == lax.rem(col // 64, 4)) & (lax.rem(row // 8, 2) == col // 256)
    pick = here & (hit > 0.5) & (place_of == lax.rem(row, 4))
    sel[...] = jnp.where(pick, 1.0, 0.0).astype(BF16)
    row = lax.broadcasted_iota(jnp.int32, (16, 64), 0)
    first = lax.rem(row // 4, 2) == 0
    hit = jnp.where(first, mine[0][0], mine[1][0])
    place_of = jnp.where(first, mine[0][1], mine[1][1]).astype(jnp.int32)
    pick = (row // 8 == zm) & (hit > 0.5) & (place_of == lax.rem(row, 4))
    own_slots = jnp.where(pick, 1.0, 0.0).astype(BF16)


    def key_block(i):
        links.arrived(kb.at[:, zs[4 - i] * 4 + y], keys_z + i - 1, at_z(zs[4 - i]))
        keys_y[4 - i].start()

    key_block(1)
    keys_y[0].forward()
    vu_y.finish()
    vu_x.start()
    key_block(2)
    keys_y[3].forward()
    key_block(3)

    keys_y[2].forward()
    keys_y[1].forward()
    vu_x.forward()
    vu_core = links.new_recv(1)
    out_core = links.new_recv(4)
    gu_core, down_core = links.new_recv(1), links.new_recv(1)
    for i in range(4):
        links.arrived(wo.at[i, x, k], out_z + i, at_z(zs[1]))
    out_x.start()
    links.start(wo.at[:, x, k], wo.at[:, x, k], out_core, other_core)
    send_expert(0, wg_in)
    send_expert(1, wu_in)
    for i in (0, 3, 2, 1):
        keys_y[i].finish()

    slot = lax.broadcasted_iota(jnp.int32, (512, 128), 0)
    lane = lax.broadcasted_iota(jnp.int32, (512, 128), 1)
    packed = None
    first = 0
    for b in range(0, 16, 2):
        len0, len1 = lens[0, b], lens[0, b + 1]
        left = (lane < len0) & (slot == lane + first)
        right = (lane >= 64) & (lane < 64 + len1) & (slot == lane - 64 + (first + len0))
        pick = jnp.where(left & (lane < 64) | right, 1.0, 0.0).astype(BF16)
        term = dot_nn(pick, kb[0, pl.ds(b, 2)].reshape(128, 576))
        packed = term if packed is None else packed + term
        first = first + len0 + len1
    kc[...] = packed.astype(BF16)

    def attend(group):
        def step(half, carry):
            rows = qs[group, pl.ds(2 * half, 2)].reshape(256, 576)
            s1 = dot_nt(rows, kc[...])
            s2 = dot_nt(rows, kb[1].reshape(1024, 576))
            token = lax.rem(lax.broadcasted_iota(jnp.int32, (256, 1024), 0), 64)
            key = lax.broadcasted_iota(jnp.int32, (256, 1024), 1)
            s2 = jnp.where(key <= token + c * 64, s2, NEGATIVE)
            top = jnp.maximum(
                jnp.max(s1, axis=1, keepdims=True), jnp.max(s2, axis=1, keepdims=True)
            )
            p1 = jnp.exp2((s1 - top) * SCALE_LOG2)
            p2 = jnp.exp2((s2 - top) * SCALE_LOG2)
            total = jnp.sum(p1, axis=1, keepdims=True) + jnp.sum(p2, axis=1, keepdims=True)
            acc = dot_nn(p1.astype(BF16), kc[:, :512])
            acc = acc + dot_nn(p2.astype(BF16), kb[1, :, :, :512].reshape(1024, 512))
            att[group, pl.ds(2 * half, 2)] = (acc / total).astype(BF16).reshape(2, 2, 64, 512)
            return carry

        lax.fori_loop(0, 2, step, 0)

    ho_y, ho_z = links.new_recv(4), links.new_recv(4)

    def head_outputs(i):
        group = ys[i]
        for zq in range(4):
            pieces = []
            for j in range(2):
                value = jnp.concatenate([vbuf[j, r, zq, group] for r in range(4)], axis=0)
                pieces.append(dot_nn(att[group, zq, j], value).astype(BF16))
            ho[i, :, zq * 256 : (zq + 1) * 256] = jnp.concatenate(pieces, axis=1)
        links.start(ho.at[i], hb.at[zm, y], ho_z + i, at_pair(group))
        if i:
            links.start(ho.at[i], hb.at[zm, y], ho_y + i, at_y(group))
        else:
            hb[zm, y] = ho[0]

    vu_x.finish()
    links.start(vbuf.at[k], vbuf.at[k], vu_core, other_core)
    attend(ys[2])
    attend(ys[1])
    links.arrived(vbuf.at[1 - k], vu_core, other_core)
    head_outputs(2)
    head_outputs(1)
    attend(ys[3])
    head_outputs(3)
    attend(ys[0])
    head_outputs(0)
    out_x.forward()
    for i in (1, 3):
        links.start(wo.at[:, xs[i], k], wo.at[:, xs[i], k], out_core + i, other_core)
    got_expert(0)
    got_expert(1)

    rs_a, rs_b, rs_z = links.new_recv(8), links.new_recv(8), links.new_recv(4)
    tiles = (0, 1, 3, 2)

    def project(n):
        i = tiles[n]
        acc = None
        for zq in range(4):
            term = dot_nt(
                hb[:, :, :, zq * 256 : (zq + 1) * 256].reshape(512, 256),
                wo[zq, xs[i]].reshape(896, 256),
            )
            acc = term if acc is None else acc + term
        part[n] = acc.astype(BF16).reshape(2, 4, 64, 896)
        links.start(part.at[n, 0, ys[2]], rsa.at[n, 0], rs_a + 2 * n, at_y(ys[1]))
        links.start(part.at[n, 1, ys[2]], rsa.at[n, 1], rs_a + 2 * n + 1, at_y(ys[3]))

    def pass_on(n):
        links.arrived(rsa.at[n, 0], rs_a + 2 * n, at_y(ys[3]))
        part[n, 0, ys[1]] = (part[n, 0, ys[1]].astype(F32) + rsa[n, 0].astype(F32)).astype(BF16)
        links.start(part.at[n, :, ys[1]], rsb.at[n, 0], rs_b + 2 * n, at_y(ys[1]))
        links.arrived(rsa.at[n, 1], rs_a + 2 * n + 1, at_y(ys[1]))
        part[n, 1, ys[3]] = (part[n, 1, ys[3]].astype(F32) + rsa[n, 1].astype(F32)).astype(BF16)
        links.start(part.at[n, :, ys[3]], rsb.at[n, 1], rs_b + 2 * n + 1, at_y(ys[3]))

    def columns(half, n):
        return pl.ds(pl.multiple_of(half * 3584 + xs[tiles[n]] * 896, 128), 896)

    def collect(n):
        links.arrived(rsb.at[n, 0], rs_b + 2 * n, at_y(ys[3]))
        links.arrived(rsb.at[n, 1], rs_b + 2 * n + 1, at_y(ys[1]))

        def total(member):
            return (
                part[n, member, y].astype(F32)
                + rsb[n, 0, member].astype(F32)
                + rsb[n, 1, member].astype(F32)
            )

        zsend[n] = total(1 - zm).astype(BF16)
        links.start(zsend.at[n], zrecv.at[n], rs_z + n, pair)
        cols = columns(zm, n)
        mixed[:, cols] = hid[:, cols].astype(F32) + total(zm)

    def slot_tile(n):
        i = tiles[n]
        links.arrived(wo.at[:, xs[i], 1 - k], out_core + i, other_core)
        acc = None
        for zq in range(4):
            term = dot_nt(hs[:, zq * 256 : (zq + 1) * 256], wo[zq, xs[i]].reshape(896, 256))
            acc = term if acc is None else acc + term
        sp[:, xs[i]] = acc.astype(BF16).reshape(4, 16, 896)

    for i in (2, 1, 3, 0):
        source = ys[(4 - i) % 4]
        if i:
            links.arrived(hb.at[zm, source], ho_y + i, at_y(source))
        links.arrived(hb.at[1 - zm, source], ho_z + i, at_pair(source))
    hs[...] = dot_nn(sel[...], hb[...].reshape(512, 1024)).astype(BF16)
    slot_tile(0)
    project(0)
    slot_tile(1)
    slot_tile(2)
    out_x.finish()
    links.start(wo.at[:, xs[2], k], wo.at[:, xs[2], k], out_core + 2, other_core)
    gu_x.start()
    send_expert(2, wd_in)
    slot_tile(3)
    slot_y, slot_z = links.new_recv(3), links.new_recv(1)
    for i in (1, 2, 3):
        links.start(sp.at[ys[i]], sq.at[i - 1], slot_y + i - 1, at_y(ys[i]))
    project(1)
    for i in (1, 2, 3):
        links.arrived(sq.at[i - 1], slot_y + i - 1, at_y(ys[4 - i]))
    half = sp[y].astype(F32) + sq[0].astype(F32) + sq[1].astype(F32) + sq[2].astype(F32)
    sx[...] = half.astype(BF16)
    links.start(sx, sy, slot_z, pair)
    nrm[zm] = half
    pass_on(0)
    project(2)
    links.arrived(sy, slot_z, pair)
    nrm[1 - zm] = sy[...].astype(F32)
    square = None
    for r in range(8):
        cols = slice(r * 896, (r + 1) * 896)
        block = nrm[r // 4, r % 4] + dot_nn(own_slots, hid[:, cols])
        nrm[r // 4, r % 4] = block
        term = jnp.sum(block * block, axis=1, keepdims=True)
        square = term if square is None else square + term
    inverse = lax.rsqrt(square * (1.0 / 7168.0) + EPSILON)
    row = lax.broadcasted_iota(jnp.int32, (16, 16), 0)
    col = lax.broadcasted_iota(jnp.int32, (16, 16), 1)
    blocks = [None, None]
    for p in range(4):
        pieces = []
        for r in (2 * p, 2 * p + 1):
            cols = slice(r * 896, (r + 1) * 896)
            pieces.append((nrm[r // 4, r % 4] * inverse * gain[:, cols]).astype(BF16))
        rows = jnp.concatenate(pieces, axis=1)
        for e in range(2):
            pick = (row // 4 == p) & (col == zm * 8 + e * 4 + lax.rem(row, 4))
            term = dot_nn(jnp.where(pick, 1.0, 0.0).astype(BF16), rows)
            blocks[e] = term if blocks[e] is None else blocks[e] + term
    for e in range(2):
        sb[e] = blocks[e].astype(BF16)
    sl_z = links.new_recv(3)
    for i in (1, 2, 3):
        links.start(sb.at[1 - zs[i] // 2], sblk.at[z], sl_z + i - 1, at_z(zs[i]))
    sblk[z] = sb[expert]
    pass_on(1)
    collect(0)
    gu_x.forward()
    got_expert(2)
    down_x.start()
    for i in (1, 2, 3):
        links.arrived(sblk.at[zs[4 - i]], sl_z + i - 1, at_z(zs[4 - i]))
    stacked = sblk[...].reshape(64, 1792)
    row = lax.broadcasted_iota(jnp.int32, (16, 64), 0)
    col = lax.broadcasted_iota(jnp.int32, (16, 64), 1)
    same = (row // 4 == col // 16) & (lax.rem(row, 4) == lax.rem(col, 4))
    for p in range(4):
        pick = jnp.where(same & (lax.rem(col, 16) // 4 == p), 1.0, 0.0).astype(BF16)
        yb[y, p] = dot_nn(pick, stacked).astype(BF16)
    sl_y = Ring(
        links, y, at_y,
        lambda o: yb.at[o],
        lambda o, j: yb.at[o, pl.ds(2 * j, 2)],
    )
    sl_y.start()
    pass_on(2)
    sl_y.forward()
    gu_x.finish()
    ready = wbuf.at[pl.ds(0, 2), :, :, k]
    links.start(ready, ready, gu_core, other_core)
    sl_y.finish()
    down_x.forward()
    project(3)
    links.arrived(wbuf.at[pl.ds(0, 2), :, :, 1 - k], gu_core, other_core)

    gate_acc = up_acc = None
    for p in range(4):
        rows = yb[:, p].reshape(64, 1792)
        span_x = pl.ds(2 * (p % 2), 2)
        g_term = dot_nn(rows, wbuf[0, p // 2, span_x].reshape(1792, 256))
        u_term = dot_nn(rows, wbuf[1, p // 2, span_x].reshape(1792, 256))
        gate_acc = g_term if gate_acc is None else gate_acc + g_term
        up_acc = u_term if up_acc is None else up_acc + u_term
    down_x.finish()
    links.start(wbuf.at[2, :, :, k], wbuf.at[2, :, :, k], down_core, other_core)
    act = (gate_acc / (1.0 + jnp.exp(-gate_acc)) * up_acc).astype(BF16)
    collect(1)
    pass_on(3)
    links.arrived(wbuf.at[2, :, :, 1 - k], down_core, other_core)
    for p in range(4):
        down = dot_nt(act, wbuf[2, p // 2, pl.ds(2 * (p % 2), 2)].reshape(1792, 256))
        dp[:, p] = down.astype(BF16).reshape(4, 16, 1792)

    d_a, d_b = links.new_recv(2), links.new_recv(2)
    links.start(dp.at[ys[2], pl.ds(0, 2)], dpa.at[0], d_a, at_y(ys[1]))
    links.start(dp.at[ys[2], pl.ds(2, 2)], dpa.at[1], d_a + 1, at_y(ys[3]))
    collect(2)
    links.arrived(dpa.at[0], d_a, at_y(ys[3]))
    head = pl.ds(0, 2)
    dp[ys[1], head] = (dp[ys[1], head].astype(F32) + dpa[0].astype(F32)).astype(BF16)
    links.start(dp.at[ys[1]], dpb.at[0], d_b, at_y(ys[1]))
    links.arrived(dpa.at[1], d_a + 1, at_y(ys[1]))
    tail = pl.ds(2, 2)
    dp[ys[3], tail] = (dp[ys[3], tail].astype(F32) + dpa[1].astype(F32)).astype(BF16)
    links.start(dp.at[ys[3]], dpb.at[1], d_b + 1, at_y(ys[3]))
    collect(3)
    links.arrived(dpb.at[0], d_b, at_y(ys[3]))
    links.arrived(dpb.at[1], d_b + 1, at_y(ys[1]))
    row = lax.broadcasted_iota(jnp.int32, (64, 16), 0)
    col = lax.broadcasted_iota(jnp.int32, (64, 16), 1)
    same = (row // 16 == col // 4) & (lax.rem(row, 4) == lax.rem(col, 4))
    blocks = None
    for p in range(4):
        total = dp[y, p].astype(F32) + dpb[0, p].astype(F32) + dpb[1, p].astype(F32)
        pick = jnp.where(same & (lax.rem(row, 16) // 4 == p), 1.0, 0.0).astype(BF16)
        term = dot_nn(pick, total.astype(BF16))
        blocks = term if blocks is None else blocks + term
    zb[...] = blocks.astype(BF16).reshape(4, 16, 1792)
    d_z = links.new_recv(3)
    for i in (1, 2, 3):
        links.start(zb.at[zs[i]], zr.at[z], d_z + i - 1, at_z(zs[i]))
    zr[z] = zb[z]
    for n in range(4):
        links.arrived(zrecv.at[n], rs_z + n, pair)
        cols = columns(1 - zm, n)
        mixed[:, cols] = hid[:, cols].astype(F32) + zrecv[n].astype(F32)
    for i in (1, 2, 3):
        links.arrived(zr.at[zs[4 - i]], d_z + i - 1, at_z(zs[4 - i]))

    for e in range(2):
        rows = zr[2 - 2 * e].astype(F32) + zr[3 - 2 * e].astype(F32)
        sblk[e] = (rows * gates[e]).astype(BF16)
    for p in range(4):
        cols = slice(p * 1792, (p + 1) * 1792)
        value = mixed[:, cols]
        for e in range(2):
            pick = jnp.transpose(chosen[4 * e + p])[:, :16].astype(BF16)
            value = value + dot_nn(pick, sblk[e])
        out[:, cols] = value.astype(BF16)

    links.finish()
    for own, remote in out_sends:

        @pl.when(jnp.logical_not(own))
        def _():
            remote().wait_send()


def body(
    hidden_in, queries, span_latent, cache_latent, cache_len, value_up, out_proj, norm_gain,
    expert_gate, expert_up, expert_down, routes, route_weights,
):
    vmem = pl.BlockSpec(memory_space=pltpu.VMEM)
    hbm = pl.BlockSpec(memory_space=pl.ANY)
    smem = pl.BlockSpec(memory_space=pltpu.SMEM)
    result = pl.pallas_call(
        kernel,
        out_shape=jax.ShapeDtypeStruct((64, 7168), BF16),
        in_specs=[smem, hbm, hbm, hbm, hbm, vmem, hbm, hbm, hbm, hbm, hbm, hbm, hbm],
        out_specs=vmem,
        scratch_shapes=[
            pltpu.VMEM((2, 16, 64, 576), BF16),
            pltpu.VMEM((512, 576), BF16),
            pltpu.VMEM((4, 4, 2, 64, 576), BF16),
            pltpu.VMEM((2, 4, 4, 4, 128, 128), BF16),
            pltpu.VMEM((3, 2, 4, 2, 448, 256), BF16),
            pltpu.VMEM((4, 4, 2, 448, 256), BF16),
            pltpu.VMEM((4, 4, 2, 64, 512), BF16),
            pltpu.VMEM((4, 64, 1024), BF16),
            pltpu.VMEM((2, 4, 64, 1024), BF16),
            pltpu.VMEM((4, 2, 4, 64, 896), BF16),
            pltpu.VMEM((4, 2, 64, 896), BF16),
            pltpu.VMEM((4, 2, 2, 64, 896), BF16),
            pltpu.VMEM((4, 64, 896), BF16),
            pltpu.VMEM((4, 64, 896), BF16),
            pltpu.VMEM((64, 7168), F32),
            pltpu.VMEM((64, 512), BF16),
            pltpu.VMEM((64, 1024), BF16),
            pltpu.VMEM((4, 4, 16, 896), BF16),
            pltpu.VMEM((3, 4, 16, 896), BF16),
            pltpu.VMEM((4, 16, 896), BF16),
            pltpu.VMEM((4, 16, 896), BF16),
            pltpu.VMEM((2, 4, 16, 896), F32),
            pltpu.VMEM((2, 16, 1792), BF16),
            pltpu.VMEM((4, 16, 1792), BF16),
            pltpu.VMEM((4, 4, 16, 1792), BF16),
            pltpu.VMEM((4, 4, 16, 1792), BF16),
            pltpu.VMEM((2, 2, 16, 1792), BF16),
            pltpu.VMEM((2, 4, 16, 1792), BF16),
            pltpu.VMEM((4, 16, 1792), BF16),
            pltpu.VMEM((4, 16, 1792), BF16),
            pltpu.VMEM((64, 7168), BF16),
            pltpu.VMEM((64, 18432), BF16),
            pltpu.VMEM((8, 1024), jnp.int32),
            pltpu.VMEM((8, 1024), F32),
            pltpu.SemaphoreType.DMA((N_SEND,)),
            pltpu.SemaphoreType.DMA((N_RECV,)),
            pltpu.SemaphoreType.DMA((8,)),
        ],
        compiler_params=pltpu.CompilerParams(
            collective_id=0, has_side_effects=True, vmem_limit_bytes=60 * 1024 * 1024
        ),
        name="layer",
    )(
        cache_len, hidden_in[0], queries[0], span_latent[0], cache_latent[0],
        norm_gain[None], routes[0].T, route_weights[0].T,
        value_up, out_proj, expert_gate, expert_up, expert_down,
    )
    return result[None]


def solution(mesh):
    in_specs = (
        P("fsdp", "ctx", None),
        P("fsdp", "ctx", None),
        P("fsdp", "ctx", None),
        P("fsdp", "ctx", None),
        P("fsdp", None),
        P("ctx", None, None),
        P("fsdp", "ctx"),
        P(),
        P("fsdp", "ctx"),
        P("fsdp", "ctx"),
        P("fsdp", "ctx"),
        P("fsdp", None, None),
        P("fsdp", None, None),
    )
    out_specs = P("fsdp", "ctx", None)
    return jax.shard_map(body, mesh=mesh, in_specs=in_specs, out_specs=out_specs, check_vma=False)
```

```python
import functools

import jax
import jax.numpy as jnp
from jax import lax
from jax.experimental import pallas as pl
from jax.experimental.pallas import tpu as pltpu
from jax.sharding import PartitionSpec as P

MESH = pl.DeviceIdType.MESH
F32 = jnp.float32
BF16 = jnp.bfloat16

CAP = 4
SCALE_LOG2 = 192.0 ** (-0.5) * 1.4426950408889634
EPSILON = 1e-06
NEGATIVE = -1e30
N_SEND = 128
N_RECV = 128


def dot_nt(a, b):
    return lax.dot_general(a, b, (((1,), (1,)), ((), ())), preferred_element_type=F32)


def dot_nn(a, b):
    return jnp.dot(a, b, preferred_element_type=F32)


class Links:
    def __init__(self, send, recv):
        self.send, self.recv = send, recv
        self.n_send = self.n_recv = 0
        self.open = []

    def new_recv(self, count=1):
        base = self.n_recv
        self.n_recv += count
        assert self.n_recv <= N_RECV
        return base

    def start(self, src, dst, recv_index, device):
        copy = pltpu.make_async_remote_copy(
            src_ref=src,
            dst_ref=dst,
            send_sem=self.send.at[self.n_send],
            recv_sem=self.recv.at[recv_index],
            device_id=device,
            device_id_type=MESH,
        )
        self.n_send += 1
        assert self.n_send <= N_SEND
        copy.start()
        self.open.append(copy)

    def arrived(self, dst, recv_index, device):
        pltpu.make_async_remote_copy(
            src_ref=dst,
            dst_ref=dst,
            send_sem=self.send.at[0],
            recv_sem=self.recv.at[recv_index],
            device_id=device,
            device_id_type=MESH,
        ).wait_recv()

    def finish(self):
        for copy in self.open:
            copy.wait_send()


class Ring:
    def __init__(self, links, at, device, chunk, half):
        self.links, self.at, self.device = links, at, device
        self.chunk, self.half = chunk, half
        self.base = links.new_recv(4)
        self.up, self.down, self.far = (lax.rem(at + i, 4) for i in (1, 3, 2))

    def start(self):
        own = self.chunk(self.at)
        self.links.start(own, own, self.base, self.device(self.up))
        self.links.start(own, own, self.base + 1, self.device(self.down))

    def forward(self):
        self.links.arrived(self.chunk(self.down), self.base, self.device(self.down))
        part = self.half(self.down, 0)
        self.links.start(part, part, self.base + 2, self.device(self.up))
        self.links.arrived(self.chunk(self.up), self.base + 1, self.device(self.up))
        part = self.half(self.up, 1)
        self.links.start(part, part, self.base + 3, self.device(self.down))

    def finish(self):
        self.links.arrived(self.half(self.far, 0), self.base + 2, self.device(self.down))
        self.links.arrived(self.half(self.far, 1), self.base + 3, self.device(self.up))


def kernel(
    lens, hid_in, q_in, span, cache, gain, routes_in, weights_in,
    vu_in, wo_in, wg_in, wu_in, wd_in,
    out,
    kb, kc, qs, vbuf, wbuf, wo, att, ho, hb,
    part, rsa, rsb, zsend, zrecv, mixed, sel, hs, sp, sq, sx, sy, nrm,
    sb, sblk, yb, dp, dpa, dpb, zb, zr, hid, q, routes, weights,
    send_sems, recv_sems, local_sems,
):
    c, f = lax.axis_index("ctx"), lax.axis_index("fsdp")
    z, y = c // 4, lax.rem(c, 4)
    zh, x, k = f // 8, lax.rem(f // 2, 4), lax.rem(f, 2)
    zm = lax.rem(z, 2)
    place_z = zh * 4 + z
    expert = 1 - z // 2
    links = Links(send_sems, recv_sems)

    def at_z(z2):
        return {"ctx": z2 * 4 + y, "fsdp": f}

    def at_y(y2):
        return {"ctx": z * 4 + y2, "fsdp": f}

    def at_x(x2):
        return {"ctx": c, "fsdp": zh * 8 + x2 * 2 + k}

    def at_zh(z2, zh2):
        return {"ctx": z2 * 4 + y, "fsdp": zh2 * 8 + x * 2 + k}

    other_core = {"ctx": c, "fsdp": zh * 8 + x * 2 + (1 - k)}
    up_two, down_two = lax.rem(place_z + 2, 8), lax.rem(place_z + 6, 8)
    twos = [at_zh(lax.rem(p, 4), p // 4) for p in (up_two, down_two)]
    partner = z + 1 - 2 * zm
    pair = at_z(partner)

    def at_pair(y2):
        return {"ctx": partner * 4 + y2, "fsdp": f}

    zs = [lax.rem(z + i, 4) for i in range(4)]
    ys = [lax.rem(y + i, 4) for i in range(4)]
    xs = [lax.rem(x + i, 4) for i in range(4)]

    local = []

    def place(src, dst):
        copy = pltpu.make_async_copy(src, dst, local_sems.at[len(local)])
        copy.start()
        local.append(copy)

    place(cache, kb.at[0, c])
    place(span, kb.at[1, c])
    place(vu_in.at[k, pl.ds(pl.multiple_of(x * 128, 128), 128)], vbuf.at[k, x, z, y])
    place(q_in, q)
    place(hid_in, hid)
    place(routes_in, routes)
    place(weights_in, weights)

    barrier = pltpu.get_barrier_semaphore()
    peers = [at_y(ys[i]) for i in (1, 2, 3)] + [at_x(xs[i]) for i in (1, 2, 3)] + [other_core]
    peers += [at_zh(zs[i], zh) for i in (1, 2, 3)] + [at_zh(zs[i], 1 - zh) for i in range(4)]
    peers += [at_pair(ys[i]) for i in (1, 2, 3)]
    for peer in peers:
        pl.semaphore_signal(barrier, inc=1, device_id=peer, device_id_type=MESH)
    pl.semaphore_wait(barrier, len(peers))
    for copy in local[:3]:
        copy.wait()

    vu_z = links.new_recv(3)
    for i in (1, 2, 3):
        own = vbuf.at[k, x, z, y]
        links.start(own, own, vu_z + i - 1, at_z(zs[i]))
    keys_z = links.new_recv(3)
    for i in (1, 2, 3):
        links.start(kb.at[:, c], kb.at[:, c], keys_z + i - 1, at_z(zs[i]))
    out_z = links.new_recv(4)
    out_sends = []
    for a in range(2):
        for b in range(2):
            z2 = zh + 2 * a
            own = (z2 == z) & (zh == b)
            sem = links.n_send
            links.n_send += 1

            def remote(sem=sem, z2=z2, b=b):
                return pltpu.make_async_remote_copy(
                    src_ref=wo_in,
                    dst_ref=wo.at[z, x, k],
                    send_sem=send_sems.at[sem],
                    recv_sem=recv_sems.at[out_z + z],
                    device_id=at_zh(z2, b),
                    device_id_type=MESH,
                )

            @pl.when(own)
            def _():
                pltpu.make_async_copy(wo_in, wo.at[z, x, k], recv_sems.at[out_z + z]).start()

            @pl.when(jnp.logical_not(own))
            def _():
                remote().start()

            out_sends.append((own, remote))

    keys_y = []
    for i in range(4):
        zi = zs[i]
        keys_y.append(
            Ring(
                links, y, at_y,
                lambda o, zi=zi: kb.at[:, zi * 4 + o],
                lambda o, j, zi=zi: kb.at[j, zi * 4 + o],
            )
        )
    keys_y[0].start()
    vu_y = Ring(
        links, y, at_y,
        lambda o: vbuf.at[k, x, :, o],
        lambda o, j: vbuf.at[k, x, pl.ds(2 * j, 2), o],
    )
    vu_x = Ring(
        links, x, at_x,
        lambda o: vbuf.at[k, o],
        lambda o, j: vbuf.at[k, o, pl.ds(2 * j, 2)],
    )
    gu_x = Ring(
        links, x, at_x,
        lambda o: wbuf.at[pl.ds(0, 2), :, o, k],
        lambda o, j: wbuf.at[pl.ds(0, 2), j, o, k],
    )
    down_x = Ring(
        links, x, at_x,
        lambda o: wbuf.at[2, :, o, k],
        lambda o, j: wbuf.at[2, j, o, k],
    )
    out_x = Ring(
        links, x, at_x,
        lambda o: wo.at[:, o, k],
        lambda o, j: wo.at[pl.ds(2 * j, 2), o, k],
    )
    expert_z = links.new_recv(6)

    def send_expert(w, ref):
        for p in twos:
            links.start(ref, wbuf.at[w, zh, x, k], expert_z + 2 * w + zh, p)

    def got_expert(w):
        for h in range(2):
            links.arrived(wbuf.at[w, h, x, k], expert_z + 2 * w + h, twos[0])

    def relayout(index, carry):
        zq, yq = index // 4, lax.rem(index, 4)
        cols = q[:, pl.ds(pl.multiple_of(index * 1152, 128), 1152)]
        qs[yq, zq, 0] = cols[:, :576]
        qs[yq, zq, 1] = cols[:, 576:]
        return carry

    for i in (1, 2, 3):
        links.arrived(vbuf.at[k, x, zs[4 - i], y], vu_z + i - 1, at_z(zs[4 - i]))
    vu_y.start()
    local[3].wait()
    lax.fori_loop(0, 16, relayout, 0)
    vu_y.forward()

    for copy in local[4:]:
        copy.wait()
    near = pl.ds(pl.multiple_of((c // 2) * 128, 128), 128)

    def own_tokens(ref):
        both = ref[:, near]
        return jnp.where(lax.rem(c, 2) == 1, both[:, 64:], both[:, :64])

    own_routes, own_weights = own_tokens(routes), own_tokens(weights)
    earlier = lax.broadcasted_iota(jnp.int32, (64, 64), 0) < lax.broadcasted_iota(
        jnp.int32, (64, 64), 1
    )
    earlier = jnp.where(earlier, 1.0, 0.0).astype(BF16)
    slot_row = lax.broadcasted_iota(jnp.int32, (128, 64), 0)
    chosen, gates, mine = [], [], []
    for e in range(2):
        match = own_routes == e
        hit = jnp.sum(jnp.where(match, 1.0, 0.0), axis=0, keepdims=True)
        weight = jnp.sum(jnp.where(match, own_weights, 0.0), axis=0, keepdims=True)
        within = dot_nn(jnp.broadcast_to(hit, (16, 64)).astype(BF16), earlier)[:1]
        named = (hit > 0.5) & (within.astype(jnp.int32) == lax.rem(slot_row, 4))
        mine.append((hit, within))
        for p in range(4):
            chosen.append(jnp.where(named & (slot_row // 4 == p), 1.0, 0.0))
        gates.append(
            jnp.sum(jnp.where(named & (slot_row < 16), weight, 0.0)[:16], axis=1, keepdims=True)
        )

    pair_routes = routes[:, pl.ds(pl.multiple_of((z // 2) * 512, 128), 512)]
    row = lax.broadcasted_iota(jnp.int32, (128, 128), 0)
    col = lax.broadcasted_iota(jnp.int32, (128, 128), 1)
    earlier = jnp.where((row < col) & (row // 64 == col // 64), 1.0, 0.0).astype(BF16)
    hits, places = [], []
    for e in range(2):
        hit = jnp.sum(jnp.where(pair_routes == e, 1.0, 0.0), axis=0, keepdims=True)
        wide = jnp.broadcast_to(hit, (16, 512)).astype(BF16)
        counts = [dot_nn(wide[:, i * 128 : (i + 1) * 128], earlier)[:1] for i in range(4)]
        hits.append(hit)
        places.append(jnp.concatenate(counts, axis=1))
    row = lax.broadcasted_iota(jnp.int32, (64, 512), 0)
    col = lax.broadcasted_iota(jnp.int32, (64, 512), 1)
    first = lax.rem(row // 4, 2) == 0
    hit = jnp.where(first, hits[0], hits[1])
    place_of = jnp.where(first, places[0], places[1]).astype(jnp.int32)
    here = (row // 16 == lax.rem(col // 64, 4)) & (lax.rem(row // 8, 2) == col // 256)
    pick = here & (hit > 0.5) & (place_of == lax.rem(row, 4))
    sel[...] = jnp.where(pick, 1.0, 0.0).astype(BF16)
    row = lax.broadcasted_iota(jnp.int32, (16, 64), 0)
    first = lax.rem(row // 4, 2) == 0
    hit = jnp.where(first, mine[0][0], mine[1][0])
    place_of = jnp.where(first, mine[0][1], mine[1][1]).astype(jnp.int32)
    pick = (row // 8 == zm) & (hit > 0.5) & (place_of == lax.rem(row, 4))
    own_slots = jnp.where(pick, 1.0, 0.0).astype(BF16)


    def key_block(i):
        links.arrived(kb.at[:, zs[4 - i] * 4 + y], keys_z + i - 1, at_z(zs[4 - i]))
        keys_y[4 - i].start()

    key_block(1)
    keys_y[0].forward()
    vu_y.finish()
    vu_x.start()
    key_block(2)
    keys_y[3].forward()
    key_block(3)

    keys_y[2].forward()
    keys_y[1].forward()
    vu_x.forward()
    vu_core = links.new_recv(1)
    out_core = links.new_recv(4)
    gu_core, down_core = links.new_recv(1), links.new_recv(1)
    for i in range(4):
        links.arrived(wo.at[i, x, k], out_z + i, at_z(zs[1]))
    out_x.start()
    links.start(wo.at[:, x, k], wo.at[:, x, k], out_core, other_core)
    send_expert(0, wg_in)
    for i in (0, 3, 2, 1):
        keys_y[i].finish()

    slot = lax.broadcasted_iota(jnp.int32, (512, 128), 0)
    lane = lax.broadcasted_iota(jnp.int32, (512, 128), 1)
    packed = None
    first = 0
    for b in range(0, 16, 2):
        len0, len1 = lens[0, b], lens[0, b + 1]
        left = (lane < len0) & (slot == lane + first)
        right = (lane >= 64) & (lane < 64 + len1) & (slot == lane - 64 + (first + len0))
        pick = jnp.where(left & (lane < 64) | right, 1.0, 0.0).astype(BF16)
        term = dot_nn(pick, kb[0, pl.ds(b, 2)].reshape(128, 576))
        packed = term if packed is None else packed + term
        first = first + len0 + len1
    kc[...] = packed.astype(BF16)

    def attend(group):
        def step(half, carry):
            rows = qs[group, pl.ds(2 * half, 2)].reshape(256, 576)
            s1 = dot_nt(rows, kc[...])
            s2 = dot_nt(rows, kb[1].reshape(1024, 576))
            token = lax.rem(lax.broadcasted_iota(jnp.int32, (256, 1024), 0), 64)
            key = lax.broadcasted_iota(jnp.int32, (256, 1024), 1)
            s2 = jnp.where(key <= token + c * 64, s2, NEGATIVE)
            top = jnp.maximum(
                jnp.max(s1, axis=1, keepdims=True), jnp.max(s2, axis=1, keepdims=True)
            )
            p1 = jnp.exp2((s1 - top) * SCALE_LOG2)
            p2 = jnp.exp2((s2 - top) * SCALE_LOG2)
            total = jnp.sum(p1, axis=1, keepdims=True) + jnp.sum(p2, axis=1, keepdims=True)
            acc = dot_nn(p1.astype(BF16), kc[:, :512])
            acc = acc + dot_nn(p2.astype(BF16), kb[1, :, :, :512].reshape(1024, 512))
            att[group, pl.ds(2 * half, 2)] = (acc / total).astype(BF16).reshape(2, 2, 64, 512)
            return carry

        lax.fori_loop(0, 2, step, 0)

    ho_y, ho_z = links.new_recv(4), links.new_recv(4)

    def head_outputs(i):
        group = ys[i]
        for zq in range(4):
            pieces = []
            for j in range(2):
                value = jnp.concatenate([vbuf[j, r, zq, group] for r in range(4)], axis=0)
                pieces.append(dot_nn(att[group, zq, j], value).astype(BF16))
            ho[i, :, zq * 256 : (zq + 1) * 256] = jnp.concatenate(pieces, axis=1)
        links.start(ho.at[i], hb.at[zm, y], ho_z + i, at_pair(group))
        if i:
            links.start(ho.at[i], hb.at[zm, y], ho_y + i, at_y(group))
        else:
            hb[zm, y] = ho[0]

    vu_x.finish()
    links.start(vbuf.at[k], vbuf.at[k], vu_core, other_core)
    attend(ys[2])
    attend(ys[1])
    links.arrived(vbuf.at[1 - k], vu_core, other_core)
    head_outputs(2)
    head_outputs(1)
    attend(ys[3])
    head_outputs(3)
    attend(ys[0])
    head_outputs(0)
    send_expert(1, wu_in)
    out_x.forward()
    for i in (1, 3):
        links.start(wo.at[:, xs[i], k], wo.at[:, xs[i], k], out_core + i, other_core)

    rs_a, rs_b, rs_z = links.new_recv(8), links.new_recv(8), links.new_recv(4)
    tiles = (0, 1, 3, 2)

    def project(n):
        i = tiles[n]
        acc = None
        for zq in range(4):
            term = dot_nt(
                hb[:, :, :, zq * 256 : (zq + 1) * 256].reshape(512, 256),
                wo[zq, xs[i]].reshape(896, 256),
            )
            acc = term if acc is None else acc + term
        part[n] = acc.astype(BF16).reshape(2, 4, 64, 896)
        links.start(part.at[n, 0, ys[2]], rsa.at[n, 0], rs_a + 2 * n, at_y(ys[1]))
        links.start(part.at[n, 1, ys[2]], rsa.at[n, 1], rs_a + 2 * n + 1, at_y(ys[3]))

    def pass_on(n):
        links.arrived(rsa.at[n, 0], rs_a + 2 * n, at_y(ys[3]))
        part[n, 0, ys[1]] = (part[n, 0, ys[1]].astype(F32) + rsa[n, 0].astype(F32)).astype(BF16)
        links.start(part.at[n, :, ys[1]], rsb.at[n, 0], rs_b + 2 * n, at_y(ys[1]))
        links.arrived(rsa.at[n, 1], rs_a + 2 * n + 1, at_y(ys[1]))
        part[n, 1, ys[3]] = (part[n, 1, ys[3]].astype(F32) + rsa[n, 1].astype(F32)).astype(BF16)
        links.start(part.at[n, :, ys[3]], rsb.at[n, 1], rs_b + 2 * n + 1, at_y(ys[3]))

    def columns(half, n):
        return pl.ds(pl.multiple_of(half * 3584 + xs[tiles[n]] * 896, 128), 896)

    def collect(n):
        links.arrived(rsb.at[n, 0], rs_b + 2 * n, at_y(ys[3]))
        links.arrived(rsb.at[n, 1], rs_b + 2 * n + 1, at_y(ys[1]))

        def total(member):
            return (
                part[n, member, y].astype(F32)
                + rsb[n, 0, member].astype(F32)
                + rsb[n, 1, member].astype(F32)
            )

        zsend[n] = total(1 - zm).astype(BF16)
        links.start(zsend.at[n], zrecv.at[n], rs_z + n, pair)
        cols = columns(zm, n)
        mixed[:, cols] = hid[:, cols].astype(F32) + total(zm)

    def slot_tile(n):
        i = tiles[n]
        links.arrived(wo.at[:, xs[i], 1 - k], out_core + i, other_core)
        acc = None
        for zq in range(4):
            term = dot_nt(hs[:, zq * 256 : (zq + 1) * 256], wo[zq, xs[i]].reshape(896, 256))
            acc = term if acc is None else acc + term
        sp[:, xs[i]] = acc.astype(BF16).reshape(4, 16, 896)

    for i in (2, 1, 3, 0):
        source = ys[(4 - i) % 4]
        if i:
            links.arrived(hb.at[zm, source], ho_y + i, at_y(source))
        links.arrived(hb.at[1 - zm, source], ho_z + i, at_pair(source))
    hs[...] = dot_nn(sel[...], hb[...].reshape(512, 1024)).astype(BF16)
    slot_tile(0)
    project(0)
    slot_tile(1)
    slot_tile(2)
    out_x.finish()
    links.start(wo.at[:, xs[2], k], wo.at[:, xs[2], k], out_core + 2, other_core)
    got_expert(0)
    got_expert(1)
    gu_x.start()
    send_expert(2, wd_in)
    slot_tile(3)
    slot_y, slot_z = links.new_recv(3), links.new_recv(1)
    for i in (1, 2, 3):
        links.start(sp.at[ys[i]], sq.at[i - 1], slot_y + i - 1, at_y(ys[i]))
    project(1)
    for i in (1, 2, 3):
        links.arrived(sq.at[i - 1], slot_y + i - 1, at_y(ys[4 - i]))
    half = sp[y].astype(F32) + sq[0].astype(F32) + sq[1].astype(F32) + sq[2].astype(F32)
    sx[...] = half.astype(BF16)
    links.start(sx, sy, slot_z, pair)
    nrm[zm] = half
    pass_on(0)
    project(2)
    links.arrived(sy, slot_z, pair)
    nrm[1 - zm] = sy[...].astype(F32)
    square = None
    for r in range(8):
        cols = slice(r * 896, (r + 1) * 896)
        block = nrm[r // 4, r % 4] + dot_nn(own_slots, hid[:, cols])
        nrm[r // 4, r % 4] = block
        term = jnp.sum(block * block, axis=1, keepdims=True)
        square = term if square is None else square + term
    inverse = lax.rsqrt(square * (1.0 / 7168.0) + EPSILON)
    row = lax.broadcasted_iota(jnp.int32, (16, 16), 0)
    col = lax.broadcasted_iota(jnp.int32, (16, 16), 1)
    blocks = [None, None]
    for p in range(4):
        pieces = []
        for r in (2 * p, 2 * p + 1):
            cols = slice(r * 896, (r + 1) * 896)
            pieces.append((nrm[r // 4, r % 4] * inverse * gain[:, cols]).astype(BF16))
        rows = jnp.concatenate(pieces, axis=1)
        for e in range(2):
            pick = (row // 4 == p) & (col == zm * 8 + e * 4 + lax.rem(row, 4))
            term = dot_nn(jnp.where(pick, 1.0, 0.0).astype(BF16), rows)
            blocks[e] = term if blocks[e] is None else blocks[e] + term
    for e in range(2):
        sb[e] = blocks[e].astype(BF16)
    sl_z = links.new_recv(3)
    for i in (1, 2, 3):
        links.start(sb.at[1 - zs[i] // 2], sblk.at[z], sl_z + i - 1, at_z(zs[i]))
    sblk[z] = sb[expert]
    pass_on(1)
    collect(0)
    gu_x.forward()
    got_expert(2)
    down_x.start()
    for i in (1, 2, 3):
        links.arrived(sblk.at[zs[4 - i]], sl_z + i - 1, at_z(zs[4 - i]))
    stacked = sblk[...].reshape(64, 1792)
    row = lax.broadcasted_iota(jnp.int32, (16, 64), 0)
    col = lax.broadcasted_iota(jnp.int32, (16, 64), 1)
    same = (row // 4 == col // 16) & (lax.rem(row, 4) == lax.rem(col, 4))
    for p in range(4):
        pick = jnp.where(same & (lax.rem(col, 16) // 4 == p), 1.0, 0.0).astype(BF16)
        yb[y, p] = dot_nn(pick, stacked).astype(BF16)
    sl_y = Ring(
        links, y, at_y,
        lambda o: yb.at[o],
        lambda o, j: yb.at[o, pl.ds(2 * j, 2)],
    )
    sl_y.start()
    pass_on(2)
    sl_y.forward()
    gu_x.finish()
    ready = wbuf.at[pl.ds(0, 2), :, :, k]
    links.start(ready, ready, gu_core, other_core)
    sl_y.finish()
    down_x.forward()
    project(3)
    links.arrived(wbuf.at[pl.ds(0, 2), :, :, 1 - k], gu_core, other_core)

    gate_acc = up_acc = None
    for p in range(4):
        rows = yb[:, p].reshape(64, 1792)
        span_x = pl.ds(2 * (p % 2), 2)
        g_term = dot_nn(rows, wbuf[0, p // 2, span_x].reshape(1792, 256))
        u_term = dot_nn(rows, wbuf[1, p // 2, span_x].reshape(1792, 256))
        gate_acc = g_term if gate_acc is None else gate_acc + g_term
        up_acc = u_term if up_acc is None else up_acc + u_term
    down_x.finish()
    links.start(wbuf.at[2, :, :, k], wbuf.at[2, :, :, k], down_core, other_core)
    act = (gate_acc / (1.0 + jnp.exp(-gate_acc)) * up_acc).astype(BF16)
    collect(1)
    pass_on(3)
    links.arrived(wbuf.at[2, :, :, 1 - k], down_core, other_core)
    for p in range(4):
        down = dot_nt(act, wbuf[2, p // 2, pl.ds(2 * (p % 2), 2)].reshape(1792, 256))
        dp[:, p] = down.astype(BF16).reshape(4, 16, 1792)

    d_a, d_b = links.new_recv(2), links.new_recv(2)
    links.start(dp.at[ys[2], pl.ds(0, 2)], dpa.at[0], d_a, at_y(ys[1]))
    links.start(dp.at[ys[2], pl.ds(2, 2)], dpa.at[1], d_a + 1, at_y(ys[3]))
    collect(2)
    links.arrived(dpa.at[0], d_a, at_y(ys[3]))
    head = pl.ds(0, 2)
    dp[ys[1], head] = (dp[ys[1], head].astype(F32) + dpa[0].astype(F32)).astype(BF16)
    links.start(dp.at[ys[1]], dpb.at[0], d_b, at_y(ys[1]))
    links.arrived(dpa.at[1], d_a + 1, at_y(ys[1]))
    tail = pl.ds(2, 2)
    dp[ys[3], tail] = (dp[ys[3], tail].astype(F32) + dpa[1].astype(F32)).astype(BF16)
    links.start(dp.at[ys[3]], dpb.at[1], d_b + 1, at_y(ys[3]))
    collect(3)
    links.arrived(dpb.at[0], d_b, at_y(ys[3]))
    links.arrived(dpb.at[1], d_b + 1, at_y(ys[1]))
    row = lax.broadcasted_iota(jnp.int32, (64, 16), 0)
    col = lax.broadcasted_iota(jnp.int32, (64, 16), 1)
    same = (row // 16 == col // 4) & (lax.rem(row, 4) == lax.rem(col, 4))
    blocks = None
    for p in range(4):
        total = dp[y, p].astype(F32) + dpb[0, p].astype(F32) + dpb[1, p].astype(F32)
        pick = jnp.where(same & (lax.rem(row, 16) // 4 == p), 1.0, 0.0).astype(BF16)
        term = dot_nn(pick, total.astype(BF16))
        blocks = term if blocks is None else blocks + term
    zb[...] = blocks.astype(BF16).reshape(4, 16, 1792)
    d_z = links.new_recv(3)
    for i in (1, 2, 3):
        links.start(zb.at[zs[i]], zr.at[z], d_z + i - 1, at_z(zs[i]))
    zr[z] = zb[z]
    for n in range(4):
        links.arrived(zrecv.at[n], rs_z + n, pair)
        cols = columns(1 - zm, n)
        mixed[:, cols] = hid[:, cols].astype(F32) + zrecv[n].astype(F32)
    for i in (1, 2, 3):
        links.arrived(zr.at[zs[4 - i]], d_z + i - 1, at_z(zs[4 - i]))

    for e in range(2):
        rows = zr[2 - 2 * e].astype(F32) + zr[3 - 2 * e].astype(F32)
        sblk[e] = (rows * gates[e]).astype(BF16)
    for p in range(4):
        cols = slice(p * 1792, (p + 1) * 1792)
        value = mixed[:, cols]
        for e in range(2):
            pick = jnp.transpose(chosen[4 * e + p])[:, :16].astype(BF16)
            value = value + dot_nn(pick, sblk[e])
        out[:, cols] = value.astype(BF16)

    links.finish()
    for own, remote in out_sends:

        @pl.when(jnp.logical_not(own))
        def _():
            remote().wait_send()


def body(
    hidden_in, queries, span_latent, cache_latent, cache_len, value_up, out_proj, norm_gain,
    expert_gate, expert_up, expert_down, routes, route_weights,
):
    vmem = pl.BlockSpec(memory_space=pltpu.VMEM)
    hbm = pl.BlockSpec(memory_space=pl.ANY)
    smem = pl.BlockSpec(memory_space=pltpu.SMEM)
    result = pl.pallas_call(
        kernel,
        out_shape=jax.ShapeDtypeStruct((64, 7168), BF16),
        in_specs=[smem, hbm, hbm, hbm, hbm, vmem, hbm, hbm, hbm, hbm, hbm, hbm, hbm],
        out_specs=vmem,
        scratch_shapes=[
            pltpu.VMEM((2, 16, 64, 576), BF16),
            pltpu.VMEM((512, 576), BF16),
            pltpu.VMEM((4, 4, 2, 64, 576), BF16),
            pltpu.VMEM((2, 4, 4, 4, 128, 128), BF16),
            pltpu.VMEM((3, 2, 4, 2, 448, 256), BF16),
            pltpu.VMEM((4, 4, 2, 448, 256), BF16),
            pltpu.VMEM((4, 4, 2, 64, 512), BF16),
            pltpu.VMEM((4, 64, 1024), BF16),
            pltpu.VMEM((2, 4, 64, 1024), BF16),
            pltpu.VMEM((4, 2, 4, 64, 896), BF16),
            pltpu.VMEM((4, 2, 64, 896), BF16),
            pltpu.VMEM((4, 2, 2, 64, 896), BF16),
            pltpu.VMEM((4, 64, 896), BF16),
            pltpu.VMEM((4, 64, 896), BF16),
            pltpu.VMEM((64, 7168), F32),
            pltpu.VMEM((64, 512), BF16),
            pltpu.VMEM((64, 1024), BF16),
            pltpu.VMEM((4, 4, 16, 896), BF16),
            pltpu.VMEM((3, 4, 16, 896), BF16),
            pltpu.VMEM((4, 16, 896), BF16),
            pltpu.VMEM((4, 16, 896), BF16),
            pltpu.VMEM((2, 4, 16, 896), F32),
            pltpu.VMEM((2, 16, 1792), BF16),
            pltpu.VMEM((4, 16, 1792), BF16),
            pltpu.VMEM((4, 4, 16, 1792), BF16),
            pltpu.VMEM((4, 4, 16, 1792), BF16),
            pltpu.VMEM((2, 2, 16, 1792), BF16),
            pltpu.VMEM((2, 4, 16, 1792), BF16),
            pltpu.VMEM((4, 16, 1792), BF16),
            pltpu.VMEM((4, 16, 1792), BF16),
            pltpu.VMEM((64, 7168), BF16),
            pltpu.VMEM((64, 18432), BF16),
            pltpu.VMEM((8, 1024), jnp.int32),
            pltpu.VMEM((8, 1024), F32),
            pltpu.SemaphoreType.DMA((N_SEND,)),
            pltpu.SemaphoreType.DMA((N_RECV,)),
            pltpu.SemaphoreType.DMA((8,)),
        ],
        compiler_params=pltpu.CompilerParams(
            collective_id=0, has_side_effects=True, vmem_limit_bytes=60 * 1024 * 1024
        ),
        name="layer",
    )(
        cache_len, hidden_in[0], queries[0], span_latent[0], cache_latent[0],
        norm_gain[None], routes[0].T, route_weights[0].T,
        value_up, out_proj, expert_gate, expert_up, expert_down,
    )
    return result[None]


def solution(mesh):
    in_specs = (
        P("fsdp", "ctx", None),
        P("fsdp", "ctx", None),
        P("fsdp", "ctx", None),
        P("fsdp", "ctx", None),
        P("fsdp", None),
        P("ctx", None, None),
        P("fsdp", "ctx"),
        P(),
        P("fsdp", "ctx"),
        P("fsdp", "ctx"),
        P("fsdp", "ctx"),
        P("fsdp", None, None),
        P("fsdp", None, None),
    )
    out_specs = P("fsdp", "ctx", None)
    return jax.shard_map(body, mesh=mesh, in_specs=in_specs, out_specs=out_specs, check_vma=False)
```
